768 devices in a mesh: row: 96 (over x, z, core), col: 8 (over y).
Axes of the slice: x: 4, y: 8, z: 12, core: 2. Of those that a mesh axis runs over, the one named last changes fastest.
Arguments:
- ocean: bfloat16 [96, 8, 12, 8192], P('row', 'col'), may hold values from -6 to 6
- land: int32 [96, 8, 8192], P('row', 'col'), may hold values 0 or 1
- weights: bfloat16 [96, 8, 24, 256, 128], P('row', 'col'), may hold values from -0.5 to 0.5
- col_map: int32 [96, 8, 24, 256], P('row', 'col'), may hold values from 0 to 8191
- row_map: int32 [96, 8, 24, 128], P('row', 'col'), may hold values from 0 to 2047
- dest: int32 [96, 8, 24, 1], P('row', 'col'), may hold values from 0 to 8; in each aligned block of 24 rows (0 to 23, 24 to 47, ..., all dimensions but the last counted through in order) at most 4 rows name the same one
- counts: int32 [96, 8], P('row', 'col'), may hold values from 12 to 24, as said below
- kappa: float32 [1536, 1024], P('row', 'col'), may hold values from 0.02 to 0.15
Outputs:
- smoothed: float32 [12, 1536, 1024], P(None, 'row', 'col')
The draws below stay inside these ranges and needn't reach their ends.
Inputs may be any that keep to these rules, and one draw needn't show every extreme that they name: `dest`: destination d of a block names atmosphere band (own band + d // 3 - 1) and tile column (own column + d % 3 - 1) mod 8; among the 24 blocks of one ocean tile at most 4 have the same d. Blocks numbered counts or higher are padding and their weights are to be ignored.
All inputs are finite; a program needn't handle non-finite values. No bound on the sum of `land` on one device may be relied on, other than what follows from the above.
Results may differ from the reference program's by a relative error of at most 0.00035.
Values sent between devices are 32-bit elements; how exact they have to be, the bound alone decides.
No kernel may reach another device: no remote copies, remote signals or barrier semaphores. Data moves between devices by JAX's collectives and lax.ppermute only.
A program may use at most 64 MiB of HBM per device.

```python
import math
import jax
import jax.numpy as jnp
import numpy as np
from jax import lax

F = 12
AY = 16
AX = 128
OC = 8192
NBLK = 24
BC = 256
BR = 128
CAP = 4
SWEEPS = 3
NAY = 1536
NAX = 1024
N_ROW = 96
N_COL = 8


def draw_counts(key, part):
    key = jax.random.fold_in(key, 7)
    first, second_key = jax.random.split(key)
    base = jax.random.randint(first, (N_ROW * N_COL,), NBLK // 2, NBLK + 1, dtype=jnp.int32)
    pick = jax.random.randint(second_key, (), 0, N_ROW * N_COL, dtype=jnp.int32)
    base = base.at[pick].set(NBLK)
    return base.reshape(N_ROW, N_COL)


def with_ends(values, key, low, top_value):
    shape = values.shape
    index_at = [jax.random.randint(jax.random.fold_in(key, axis), (), 0, shape[axis]) for axis in range(len(shape))]
    values = values.at[tuple(index_at)].set(low)
    longest = shape.index(max(shape))
    index_at[longest] = (index_at[longest] + 1) % shape[longest]
    return values.at[tuple(index_at)].set(top_value)


def block_scale(stream_key, dims, cuts, low, top_value):
    level = 1.0
    for position, blocks in cuts:
        draws = jax.random.uniform(jax.random.fold_in(jax.random.fold_in(stream_key, 6), position), (blocks,), jnp.float32, low / len(cuts), top_value / len(cuts))
        level = level * jnp.repeat(jnp.exp(draws), dims[position] // blocks).reshape((-1,) + (1,) * (len(dims) - 1 - position))
    return level


def shared_out(rng, own, number, rows, number_of, top, limit, slope):
    ranking = jax.random.permutation(rng, number_of)
    packed, common = load_shares(number_of, rows * top, limit, slope, True), load_shares(number_of, rows * top, limit, slope, False)
    places = jnp.arange(number_of)

    def named(sizes, offset_by):
        used = int((sizes > 0).sum())
        fixed = max(1, used // 4)
        shifted = fixed + (places - fixed + offset_by * (used - fixed)) % max(1, number_of - fixed)
        return jnp.zeros((number_of,), jnp.int32).at[ranking[jnp.where(places < fixed, places, shifted)]].set(jnp.asarray(sizes, jnp.int32))

    sizes = jnp.where(number % 4 == 0, named(packed, number // 4), named(common, number - number // 4 - 1))
    mixed = jax.random.permutation(jax.random.fold_in(own, 3), number_of)
    donor, receiver = mixed[0:number_of // 2 * 2:2], mixed[1:number_of // 2 * 2:2]
    slack = jnp.minimum(sizes[donor] - 1, limit - sizes[receiver]) // 2
    slack = jnp.where((donor == ranking[0]) | (receiver == ranking[0]) | (sizes[receiver] == 0), 0, jnp.maximum(slack, 0))
    shifted = jax.random.randint(jax.random.fold_in(own, 4), (number_of // 2,), 0, 1 << 20) % (slack + 1)
    sizes = sizes.at[donor].add(-shifted).at[receiver].add(shifted)
    items = jnp.searchsorted(jnp.cumsum(sizes), jnp.arange(rows * top), side="right").astype(jnp.int32)
    listing = items.reshape(top, rows).T
    listing = listing[jax.random.permutation(jax.random.fold_in(own, 1), rows)]
    offset_by = jax.random.randint(jax.random.fold_in(own, 2), (rows, 1), 0, top)
    return jnp.take_along_axis(listing, (jnp.arange(top)[None, :] + offset_by) % top, axis=1)


def load_shares(number_of, total, most, slope, full):
    portions = [(1 << 20) // math.isqrt(rank ** slope) + 1 for rank in range(1, number_of + 1)]
    largest = most if full else min(most, max(-(-total // number_of), total * portions[0] // sum(portions)))
    least = 1 if total - largest >= number_of - 1 else 0
    given, spare = [largest] + [least] * (number_of - 1), total - largest - least * (number_of - 1)
    while spare > 0:
        free = [i for i in range(1, number_of) if given[i] < largest] or [i for i in range(1, number_of) if given[i] < most]
        mass, remaining = sum([portions[i] for i in free]), spare
        for i in free:
            addition = min(most - given[i], max(1, remaining * portions[i] // mass), spare)
            given[i] = given[i] + addition
            spare = spare - addition
    return np.array(given)


def centred(own_key, shape, deviation, reach, shards=(), kind=jnp.bfloat16):
    array = jax.random.normal(own_key, shape, jnp.float32) * deviation
    if len(shards) > 0:
        array = block_scale(own_key, shape, shards, -0.22, 0.18) * array
    return jnp.clip(array, min=-reach, max=reach).astype(kind)


def setup_inputs(seed: int = 0) -> dict:
    keys = jax.random.split(jax.random.key(seed), 9)
    ocean = centred(keys[0], (N_ROW, N_COL, F, OC), 1.0, 6.0, ((0, 96), (1, 8)))
    land = with_ends((jax.random.randint(keys[1], (N_ROW, N_COL, OC), 0, 10) < 7).astype(jnp.int32), jax.random.fold_in(keys[1], 1), 0, 1)
    weights = centred(keys[2], (N_ROW, N_COL, NBLK, BC, BR), 128 ** -0.5, 0.5, ((0, 96), (1, 8)))
    col_map = with_ends(jax.random.randint(keys[3], (N_ROW, N_COL, NBLK, BC), 0, OC), jax.random.fold_in(keys[3], 1), 0, OC - 1).astype(jnp.int32)
    row_map = with_ends(jax.random.randint(keys[4], (N_ROW, N_COL, NBLK, BR), 0, AY * AX), jax.random.fold_in(keys[4], 1), 0, (AY * AX) - 1).astype(jnp.int32)
    dest_keys = jax.random.split(jax.random.fold_in(keys[5], 1), N_ROW * N_COL * NBLK // NBLK)
    dest_turns = jax.random.permutation(jax.random.fold_in(keys[5], 3), N_ROW * N_COL * NBLK // NBLK)
    dest = jax.vmap(lambda own, number: shared_out(jax.random.fold_in(keys[5], 2), own, number, NBLK, 9, 1, CAP, 2))(dest_keys, dest_turns).reshape((N_ROW, N_COL, NBLK, 1))
    counts = draw_counts(jax.random.fold_in(keys[8], 71), 0)
    kappa = jnp.clip(jnp.exp(math.log(0.15) - 2.014903 * jax.random.uniform(keys[7], (NAY, NAX), jnp.float32) ** block_scale(keys[7], (NAY, NAX), ((0, 96), (1, 8)), -0.2, 0.2)), 0.02, 0.15)
    return dict(ocean=ocean, land=land, weights=weights, col_map=col_map, row_map=row_map, dest=dest, counts=counts, kappa=kappa)


def second(padded, center, axis):
    size = center.shape[axis]
    plus_one = lax.slice_in_dim(padded, 3, 3 + size, axis=axis)
    minus_one = lax.slice_in_dim(padded, 1, 1 + size, axis=axis)
    plus_two = lax.slice_in_dim(padded, 4, 4 + size, axis=axis)
    minus_two = lax.slice_in_dim(padded, 0, size, axis=axis)
    return (4.0 / 3.0) * (plus_one + minus_one - 2.0 * center) - (1.0 / 12.0) * (plus_two + minus_two - 2.0 * center)


def reference(ocean, land, weights, col_map, row_map, dest, counts, kappa):
    cells = AY * AX
    own_cols = jnp.arange(N_COL, dtype=jnp.int32)[:, None]

    def band_step(atmos, band):
        fields = ocean[band].astype(jnp.float32) * land[band].astype(jnp.float32)[:, None, :]
        picked = jax.vmap(lambda one, cols: jnp.take(one, cols, axis=1))(fields, col_map[band])
        partial_value = jnp.einsum("cfbj,cbji->cbfi", picked, weights[band].astype(jnp.float32), precision=lax.Precision.HIGHEST)
        live = jnp.arange(NBLK, dtype=jnp.int32)[None, :] < counts[band][:, None]
        partial_value = partial_value * live[:, :, None, None].astype(jnp.float32)
        target = dest[band, :, :, 0]
        bands = band + target // 3
        columns = (own_cols + target % 3 - 1 + N_COL) % N_COL
        atmos = atmos.at[bands[:, :, None], columns[:, :, None], :, row_map[band]].add(jnp.swapaxes(partial_value, 2, 3))
        return atmos, None

    start = jnp.zeros((N_ROW + 2, N_COL, F, cells), jnp.float32)
    atmos = lax.scan(band_step, start, jnp.arange(N_ROW, dtype=jnp.int32))[0][1:-1]
    field = atmos.reshape(N_ROW, N_COL, F, AY, AX).transpose(2, 0, 3, 1, 4).reshape(F, N_ROW * AY, N_COL * AX)
    for sweep in range(SWEEPS):
        lat = jnp.pad(field, ((0, 0), (2, 2), (0, 0)))
        lon = jnp.pad(field, ((0, 0), (0, 0), (2, 2)), mode="wrap")
        field = field + kappa[None] * (second(lat, field, 1) + second(lon, field, 2))
    return field
```

```python
import functools

import jax
import jax.numpy as jnp
from jax import lax
from jax.experimental import pallas as pl
from jax.experimental.pallas import tpu as pltpu
from jax.sharding import PartitionSpec as P

F, AY, AX, OC, NBLK, BC, BR = 12, 16, 128, 8192, 24, 256, 128
NT = (((1,), (1,)), ((), ()))


def split2(x):
    hi = x.astype(jnp.bfloat16)
    return hi, (x - hi.astype(jnp.float32)).astype(jnp.bfloat16)


def remap_kernel(dest_in, counts_in, ocean_in, land_in, weights_in, col_in, row_in, kappa_in,
                 pack_ref, mid_ref, dest_ref, counts_ref, ocean_ref, land_ref, weight_ref, col_ref, row_ref, kappa_ref,
                 fields_ref, table_ref, partial_ref, tiles_ref, sems, *, ga, gb):
    f32, bf16, i32 = jnp.float32, jnp.bfloat16, jnp.int32
    pairs = ((land_in, land_ref), (ocean_in.at[0, 0], ocean_ref), (col_in.at[0, 0], col_ref), (weights_in.at[0, 0], weight_ref),
             (counts_in, counts_ref), (row_in.at[0, 0], row_ref), (dest_in, dest_ref), (kappa_in, kappa_ref))
    copies = [pltpu.make_async_copy(a, b, sems.at[i]) for i, (a, b) in enumerate(pairs)]
    for copy in copies:
        copy.start()
    tiles_ref[...] = jnp.zeros_like(tiles_ref)
    copies[0].wait()
    copies[1].wait()
    sea = land_ref[...].astype(f32)
    fields_ref[0:F, :] = ocean_ref[...].astype(f32) * sea
    fields_ref[F:16, :] = jnp.zeros((16 - F, OC), f32)
    high = OC // BC
    upper = fields_ref[0:8, :]
    lower = fields_ref[8:16, :]
    lower_down = pltpu.roll(lower, 4, 0)
    cut = lambda a, h: a[:, h * BC:(h + 1) * BC]
    table_ref[0:8 * high, :] = jnp.concatenate([cut(upper, h) for h in range(high)], 0).astype(bf16)
    table_ref[8 * high:12 * high, :] = jnp.concatenate(
        [cut(lower, 2 * p) + cut(lower_down, 2 * p + 1) for p in range(high // 2)], 0).astype(bf16)
    for copy in copies[2:]:
        copy.wait()
    count = counts_ref[0]
    sub = lax.broadcasted_iota(i32, (8, BC), 0)
    odd = (sub >= 4).astype(i32)
    cells = lax.broadcasted_iota(i32, (BC, BC), 0)

    def pick(b):
        col = col_ref[pl.ds(b, 1), :]
        low = jnp.bitwise_and(col, BC - 1)
        hi = jnp.right_shift(col, 8)
        onehot = (cells == low).astype(f32).astype(bf16)
        got = jnp.dot(table_ref[...], onehot, preferred_element_type=f32)
        hi8 = jnp.broadcast_to(hi, (8, BC))
        up = jnp.zeros((8, BC), f32)
        for h in range(high):
            up = jnp.where(hi8 == h, got[8 * h:8 * h + 8], up)
        pair = hi8 - odd
        down = jnp.zeros((8, BC), f32)
        for p in range(high // 2):
            down = jnp.where(pair == 2 * p, got[8 * (high + p):8 * (high + p) + 8], down)
        down = down + pltpu.roll(down, 4, 0)
        picked = jnp.concatenate([up, down], 0).astype(bf16)
        value = jnp.dot(picked, weight_ref[b], preferred_element_type=f32)
        partial_ref[b] = jnp.where(b < count, value, 0.0)

    def groups(n, one):
        def step(i, carry):
            for j in range(n):
                one(i * n + j)
            return carry
        lax.fori_loop(0, NBLK // n, step, 0)

    groups(ga, pick)
    lanes = lax.broadcasted_iota(i32, (AX, BR), 0)
    rows16 = lax.broadcasted_iota(i32, (AY, BR), 0)

    def place(b):
        cell = row_ref[pl.ds(b, 1), :]
        x = jnp.bitwise_and(cell, AX - 1)
        y = jnp.right_shift(cell, 7)
        at_x = (lanes == x).astype(f32).astype(bf16)
        at_y = rows16 == y
        value = partial_ref[b]
        head = value.astype(bf16).astype(f32)
        tail = value - head
        spread = lambda v: jnp.concatenate(
            [jnp.where(at_y, v[f:f + 1, :], 0.0) for f in range(F)], 0).astype(bf16)
        left = jnp.concatenate([spread(head), spread(tail)], 1)
        right = jnp.concatenate([at_x, at_x], 1)
        return lax.dot_general(left, right, NT, preferred_element_type=f32)

    def place_group(i, carry):
        got = [place(i * gb + j) for j in range(gb)]
        for j in range(gb):
            d = dest_ref[i * gb + j]
            tiles_ref[d] = tiles_ref[d] + got[j]
        return carry

    lax.fori_loop(0, NBLK // gb, place_group, 0)

    er = lax.broadcasted_iota(i32, (16, AX), 0)
    ec = lax.broadcasted_iota(i32, (16, AX), 1)
    edge = (ec == jnp.where(er < 8, er, er + AX - 16)).astype(f32).astype(bf16)
    edge2 = jnp.concatenate([edge, edge], 1)
    kappa = kappa_ref[...]
    for band in range(3):
        for dc in range(3):
            tile = tiles_ref[3 * band + dc]
            if dc == 1:
                tile = jnp.concatenate([tile, kappa if band == 1 else jnp.zeros((AY, AX), f32)], 0)
                mid_ref[band] = tile
            else:
                tile = jnp.concatenate([tile, jnp.zeros((AY, AX), f32)], 0)
                pack_ref[dc // 2, band, 0:F * AY, :] = tile[0:F * AY]
            hi, lo = split2(tile)
            strip = lax.dot_general(edge2, jnp.concatenate([hi, lo], 1), NT, preferred_element_type=f32)
            first = strip[:, 0:128]
            second = jnp.concatenate([strip[:, 128:], jnp.zeros((16, 256 - 13 * AY), f32)], 1)
            L = (first[0:8], second[0:8])
            R = (first[8:16], second[8:16])

            def put(side, row, pair):
                pack_ref[side, band, row:row + 8, :] = pair[0]
                pack_ref[side, band, row + 8:row + 16, :] = pair[1]
            if dc == 1:
                put(1, 192, R)
                put(0, 192, L)
            elif dc == 2:
                put(1, 208, R)
                put(1, 224, L)
            else:
                put(0, 208, L)
                put(0, 224, R)


def remap(dest, counts, ocean, land, weights, col_map, row_map, kappa, ga=24, gb=24):
    f32 = jnp.float32
    vm = pl.BlockSpec(memory_space=pltpu.VMEM)
    return pl.pallas_call(
        functools.partial(remap_kernel, ga=ga, gb=gb),
        out_shape=(jax.ShapeDtypeStruct((2, 3, 240, 128), f32), jax.ShapeDtypeStruct((3, 208, 128), f32)),
        in_specs=[pl.BlockSpec(memory_space=pltpu.HBM)] * 8,
        out_specs=(vm, vm),
        scratch_shapes=[
            pltpu.SMEM((NBLK,), jnp.int32),
            pltpu.SMEM((1,), jnp.int32),
            pltpu.VMEM((F, OC), jnp.bfloat16),
            pltpu.VMEM((1, OC), jnp.int32),
            pltpu.VMEM((NBLK, BC, BR), jnp.bfloat16),
            pltpu.VMEM((NBLK, BC), jnp.int32),
            pltpu.VMEM((NBLK, BR), jnp.int32),
            pltpu.VMEM((AY, AX), f32),
            pltpu.VMEM((16, OC), f32),
            pltpu.VMEM((384, BC), jnp.bfloat16),
            pltpu.VMEM((NBLK, 16, BR), f32),
            pltpu.VMEM((9, F * AY, AX), f32),
            pltpu.SemaphoreType.DMA((8,)),
        ],
        compiler_params=pltpu.CompilerParams(vmem_limit_bytes=32 * 1024 * 1024),
    )(dest, counts, ocean, land, weights, col_map, row_map, kappa)


SWEEPS = 3


def smooth_kernel(inside_ref, own_ref, top_ref, bottom_ref, out_ref, side_ref):
    f32 = jnp.float32
    wide = 2 * AX

    def sides(ref, row, slot):
        strip = lambda at: jnp.concatenate([ref[at:at + 8, :], ref[at + 8:at + 16, :]], 1)
        rows = jnp.concatenate([strip(row + 16), jnp.zeros((AX - 16, wide), f32), strip(row)], 0)
        side_ref[slot] = jnp.concatenate([rows[:, :AX].T, rows[:, AX:].T], 0)

    sides(own_ref, 13 * AY, 0)
    sides(top_ref, 13 * 8, 1)
    sides(bottom_ref, 13 * 8, 2)

    def extended(f):
        main = jnp.concatenate([top_ref[8 * f:8 * f + 8], own_ref[AY * f:AY * f + AY], bottom_ref[8 * f:8 * f + 8]], 0)
        halo = jnp.concatenate([side_ref[1, AY * f + 8:AY * f + 16], side_ref[0, AY * f:AY * f + AY],
                                side_ref[2, AY * f:AY * f + 8]], 0)
        return jnp.concatenate([main, halo], 1)

    rows = lax.broadcasted_iota(jnp.int32, (AY + 16, wide), 0)
    inside = jnp.logical_and(jnp.logical_or(rows >= 8, inside_ref[0] == 1),
                             jnp.logical_or(rows < 8 + AY, inside_ref[1] == 1))
    kappa = extended(F)
    for f in range(F):
        u = jnp.where(inside, extended(f), 0.0)
        for sweep in range(SWEEPS):
            roll = lambda by, dim: pltpu.roll(u, by % u.shape[dim], dim)
            near = (roll(1, 0) + roll(-1, 0)) + (roll(1, 1) + roll(-1, 1))
            far = (roll(2, 0) + roll(-2, 0)) + (roll(2, 1) + roll(-2, 1))
            u = u + kappa * (4.0 / 3.0 * near - 1.0 / 12.0 * far - 5.0 * u)
            if sweep < SWEEPS - 1:
                u = jnp.where(inside, u, 0.0)
        out_ref[f] = u[8:8 + AY, 0:AX]


def smooth(inside, own, top, bottom):
    vm = pl.BlockSpec(memory_space=pltpu.VMEM)
    return pl.pallas_call(
        smooth_kernel,
        out_shape=jax.ShapeDtypeStruct((F, AY, AX), jnp.float32),
        in_specs=[pl.BlockSpec(memory_space=pltpu.SMEM), vm, vm, vm],
        out_specs=vm,
        scratch_shapes=[pltpu.VMEM((3, 2 * AX, AX), jnp.float32)],
        compiler_params=pltpu.CompilerParams(vmem_limit_bytes=16 * 1024 * 1024),
    )(inside, own, top, bottom)


def partners(n_row, n_col):
    at = lambda r, c: (r % n_row) * n_col + c % n_col
    chip = [[at(2 * k, c), at(2 * k + 1, c)] for k in range(n_row // 2) for c in range(n_col)]
    beside = [[at(r, c), at(r, c + 1)] for r in range(n_row) for c in range(r % 2, n_col, 2)]
    bands = [[at(2 * k + 1, c), at(2 * k + 2, c)] for k in range(n_row // 2) for c in range(n_col)]
    beyond = []
    for r in range(n_row):
        for c in range(n_col):
            step = 2 if (r + c) % 2 == 0 else -2
            beyond.append((at(r, c), at(r ^ 1, c + step)))
    return chip, beside, bands, beyond


def per_device(ocean, land, weights, col_map, row_map, dest, counts, kappa):
    both = ("row", "col")
    n_row, n_col = lax.axis_size("row"), lax.axis_size("col")
    chip, beside, bands, beyond = partners(n_row, n_col)
    row, col = lax.axis_index("row"), lax.axis_index("col")
    core = row % 2
    first = core == 0
    ahead = (row + col) % 2 == 0
    side = jnp.where(ahead, 1, 0)
    swap = lambda value, groups, place: lax.dynamic_index_in_dim(
        lax.all_gather(value, both, axis_index_groups=groups), place, 0, keepdims=False)
    take = lambda value, place: lax.dynamic_index_in_dim(value, place, 0, keepdims=False)
    part = lambda value, start, size, dim: lax.dynamic_slice_in_dim(value, start, size, dim)

    packs, mid = remap(dest.reshape(NBLK), counts.reshape(1), ocean, land.reshape(1, OC), weights, col_map, row_map, kappa)
    mine = take(packs, side)
    other = swap(take(packs, 1 - side), chip, 1 - core)
    four = lambda a, b: jnp.pad(a, ((0, 1), (0, 0), (0, 0))) + jnp.pad(b, ((1, 0), (0, 0), (0, 0)))
    total = four(jnp.where(first, mine, other), jnp.where(first, other, mine))
    far = lax.ppermute(total[:, 208:224], both, beyond)
    near = swap(total[:, 0:208], beside, side)
    strip = near[:, 192:208] + far + total[:, 224:240]
    zero = jnp.zeros_like(mid)
    placed = four(jnp.where(first, mid, zero), jnp.where(first, zero, mid))
    field = placed + jnp.pad(near[:, 0:192], ((0, 0), (0, 16), (0, 0)))
    whole = jnp.concatenate([field, strip], 1)
    mine = part(whole, 2 * core, 2, 0)
    other = swap(part(whole, 2 - 2 * core, 2, 0), chip, 1 - core)
    east = jnp.where(ahead, mine[:, 208:], other[:, 208:])
    west = jnp.where(ahead, other[:, 208:], mine[:, 208:])
    main = mine[:, :208] + other[:, :208]
    half = lambda value, start: part(value[:208].reshape(13, AY, AX), start, 8, 1).reshape(104, AX)
    edges = jnp.concatenate([west, east], 1)
    mine_main, mine_edges = take(main, 1 - core), take(edges, 1 - core)
    out_main, out_edges = take(main, core), take(edges, core)
    sent = jnp.concatenate([out_main, out_edges, half(mine_main, 8 * core), mine_edges], 0)
    got = swap(sent, bands, core)
    outer = jnp.logical_or(row == 0, row == n_row - 1)
    got = jnp.where(outer, 0.0, got)
    own = jnp.concatenate([mine_main, mine_edges], 0) + got[:240]
    outside = jnp.concatenate([half(out_main, 8 - 8 * core), out_edges], 0) + got[240:]
    within = swap(jnp.concatenate([half(own, 8 - 8 * core), own[208:]], 0), chip, 1 - core)
    top = jnp.where(first, outside, within)
    bottom = jnp.where(first, within, outside)
    inside = jnp.stack([row != 0, row != n_row - 1]).astype(jnp.int32)
    return smooth(inside, own, top, bottom)


def solution(mesh):
    placed = (
        P("row", "col", None, None),
        P("row", "col", None),
        P("row", "col", None, None, None),
        P("row", "col", None, None),
        P("row", "col", None, None),
        P("row", "col", None, None),
        P("row", "col"),
        P("row", "col"),
    )
    return jax.shard_map(
        per_device, mesh=mesh, in_specs=placed, out_specs=P(None, "row", "col"), check_vma=False
    )
```

```python
import functools

import jax
import jax.numpy as jnp
from jax import lax
from jax.experimental import pallas as pl
from jax.experimental.pallas import tpu as pltpu
from jax.sharding import PartitionSpec as P

F, AY, AX, OC, NBLK, BC, BR = 12, 16, 128, 8192, 24, 256, 128
MIX = (1, 0)
NT = (((1,), (1,)), ((), ()))


def split2(x):
    hi = x.astype(jnp.bfloat16)
    return hi, (x - hi.astype(jnp.float32)).astype(jnp.bfloat16)


def remap_kernel(side_ref, dest_in, counts_in, ocean_in, land_in, weights_in, col_in, row_in, kappa_in,
                 sent_out, kept_out, mid_out, dest_ref, counts_ref, ocean_ref, land_ref, weight_ref, col_ref, row_ref, kappa_ref,
                 fields_ref, table_ref, rows_ref, partial_ref, tiles_ref, strips_ref, extra_ref, sems, out_sems, *, ga, gb):
    f32, bf16, i32 = jnp.float32, jnp.bfloat16, jnp.int32
    pairs = ((land_in, land_ref), (ocean_in.at[0, 0], ocean_ref), (col_in.at[0, 0], col_ref), (weights_in.at[0, 0], weight_ref),
             (counts_in, counts_ref), (row_in.at[0, 0], row_ref), (dest_in, dest_ref), (kappa_in, kappa_ref))
    copies = [pltpu.make_async_copy(a, b, sems.at[i]) for i, (a, b) in enumerate(pairs)]
    for copy in copies:
        copy.start()
    tiles_ref[...] = jnp.zeros_like(tiles_ref)
    copies[0].wait()
    copies[1].wait()
    sea = land_ref[...].astype(f32)
    high = OC // 128
    fields_ref[0:8, :] = ocean_ref[0:8, :].astype(f32) * sea
    fields_ref[8:12, :] = ocean_ref[8:12, :].astype(f32) * sea
    fields_ref[12:16, :] = jnp.zeros((4, OC), f32)
    low8 = fields_ref[8:16, :]
    down8 = pltpu.roll(low8, 4, 0)
    blocks = OC // BC
    cut = lambda a, h: a[:, h * BC:(h + 1) * BC]
    upper = fields_ref[0:8, :]
    rows_ref[0:8 * blocks, :] = jnp.concatenate([cut(upper, h) for h in range(blocks)], 0).astype(bf16)
    rows_ref[8 * blocks:12 * blocks, :] = jnp.concatenate(
        [cut(low8, 2 * p) + cut(down8, 2 * p + 1) for p in range(blocks // 2)], 0).astype(bf16)
    for p in range(high // 2):
        table_ref[:, p * 128:(p + 1) * 128] = low8[:, 256 * p:256 * p + 128] + down8[:, 256 * p + 128:256 * p + 256]
    for copy in copies[2:]:
        copy.wait()
    count = counts_ref[0]
    odd = (lax.broadcasted_iota(i32, (8, 128), 0) >= 4).astype(i32)

    def finish(b, up, down):
        picked = jnp.concatenate([up, down], 0).astype(bf16)
        value = jnp.dot(picked, weight_ref[b], preferred_element_type=f32)
        partial_ref[b] = jnp.where(b < count, value, 0.0)

    cells = lax.broadcasted_iota(i32, (BC, BC), 0)
    odd2 = (lax.broadcasted_iota(i32, (8, BC), 0) >= 4).astype(i32)

    def pick_dot(b):
        col = col_ref[pl.ds(b, 1), :]
        low = jnp.bitwise_and(col, BC - 1)
        hi = jnp.right_shift(col, 8)
        onehot = (cells == low).astype(f32).astype(bf16)
        got = jnp.dot(rows_ref[...], onehot, preferred_element_type=f32)
        hi8 = jnp.broadcast_to(hi, (8, BC))
        up = jnp.zeros((8, BC), f32)
        for h in range(blocks):
            up = jnp.where(hi8 == h, got[8 * h:8 * h + 8], up)
        pair = hi8 - odd2
        down = jnp.zeros((8, BC), f32)
        for p in range(blocks // 2):
            down = jnp.where(pair == 2 * p, got[8 * (blocks + p):8 * (blocks + p) + 8], down)
        down = down + pltpu.roll(down, 4, 0)
        finish(b, up, down)

    def pick(b):
        ups, downs = [], []
        for t in range(BC // 128):
            col = jnp.broadcast_to(col_ref[pl.ds(b, 1), :][:, 128 * t:128 * t + 128], (8, 128))
            low = jnp.bitwise_and(col, 127)
            hi8 = jnp.right_shift(col, 7)
            up = jnp.zeros((8, 128), f32)
            for h in range(high):
                got = jnp.take_along_axis(fields_ref[0:8, 128 * h:128 * h + 128], low, 1)
                up = jnp.where(hi8 == h, got, up)
            pair = hi8 - odd
            down = jnp.zeros((8, 128), f32)
            for p in range(high // 2):
                got = jnp.take_along_axis(table_ref[:, 128 * p:128 * p + 128], low, 1)
                down = jnp.where(pair == 2 * p, got, down)
            ups.append(up)
            downs.append(down + pltpu.roll(down, 4, 0))
        up = jnp.concatenate(ups, 1)
        down = jnp.concatenate(downs, 1)
        finish(b, up, down)

    def groups(n, one):
        def step(i, carry):
            for j in range(n):
                (one if MIX[j % len(MIX)] else pick_dot)(i * n + j)
            return carry
        lax.fori_loop(0, NBLK // n, step, 0)

    groups(ga, pick)
    lanes = lax.broadcasted_iota(i32, (AX, BR), 0)
    rows16 = lax.broadcasted_iota(i32, (AY, BR), 0)

    def place(b):
        cell = row_ref[pl.ds(b, 1), :]
        x = jnp.bitwise_and(cell, AX - 1)
        y = jnp.right_shift(cell, 7)
        at_x = (lanes == x).astype(f32).astype(bf16)
        at_y = rows16 == y
        value = partial_ref[b]
        head = value.astype(bf16).astype(f32)
        tail = value - head
        spread = lambda v: jnp.concatenate(
            [jnp.where(at_y, v[f:f + 1, :], 0.0) for f in range(F)], 0).astype(bf16)
        left = jnp.concatenate([spread(head), spread(tail)], 1)
        right = jnp.concatenate([at_x, at_x], 1)
        return lax.dot_general(left, right, NT, preferred_element_type=f32)

    def place_group(i, carry):
        got = [place(i * gb + j) for j in range(gb)]
        for j in range(gb):
            d = dest_ref[i * gb + j]
            slot = 3 * lax.rem(d, 3) + lax.div(d, 3)
            tiles_ref[slot] = tiles_ref[slot] + got[j]
        return carry

    lax.fori_loop(0, NBLK // gb, place_group, 0)

    side = side_ref[0]
    outs = []

    def out(source, target):
        outs.append(pltpu.make_async_copy(source, target, out_sems.at[len(outs)]))
        outs[-1].start()

    main = F * AY
    out(tiles_ref.at[pl.ds(6 - 6 * side, 3)], sent_out.at[:, 0:main])
    out(tiles_ref.at[pl.ds(6 * side, 3)], kept_out.at[:, 0:main])
    out(tiles_ref.at[pl.ds(3, 3)], mid_out.at[:, 0:main])
    er = lax.broadcasted_iota(i32, (16, AX), 0)
    ec = lax.broadcasted_iota(i32, (16, AX), 1)
    edge = (ec == jnp.where(er < 8, er, er + AX - 16)).astype(f32).astype(bf16)
    edge2 = jnp.concatenate([edge, edge], 1)
    kappa = kappa_ref[...]
    extra_ref[...] = jnp.zeros_like(extra_ref)
    extra_ref[1] = kappa
    out(extra_ref, mid_out.at[:, main:main + AY])
    for band in range(3):
        for dc in range(3):
            tile = jnp.concatenate([tiles_ref[3 * dc + band], kappa if 3 * dc + band == 4 else jnp.zeros((AY, AX), f32)], 0)
            hi, lo = split2(tile)
            strip = lax.dot_general(edge2, jnp.concatenate([hi, lo], 1), NT, preferred_element_type=f32)
            first = strip[:, 0:128]
            second = jnp.concatenate([strip[:, 128:], jnp.zeros((16, 256 - 13 * AY), f32)], 1)
            west = jnp.concatenate([first[0:8], second[0:8]], 0)
            east = jnp.concatenate([first[8:16], second[8:16]], 0)
            if dc == 1:
                strips_ref[1, band, 0:16] = east
                strips_ref[0, band, 0:16] = west
            elif dc == 2:
                strips_ref[1, band, 16:32] = east
                strips_ref[1, band, 32:48] = west
            else:
                strips_ref[0, band, 16:32] = west
                strips_ref[0, band, 32:48] = east
    out(strips_ref.at[1 - side], sent_out.at[:, main:main + 48])
    out(strips_ref.at[side], kept_out.at[:, main:main + 48])
    for copy in outs:
        copy.wait()


def remap(side, dest, counts, ocean, land, weights, col_map, row_map, kappa, ga=12, gb=24):
    f32 = jnp.float32
    return pl.pallas_call(
        functools.partial(remap_kernel, ga=ga, gb=gb),
        out_shape=(jax.ShapeDtypeStruct((3, 240, 128), f32), jax.ShapeDtypeStruct((3, 240, 128), f32), jax.ShapeDtypeStruct((3, 208, 128), f32)),
        in_specs=[pl.BlockSpec(memory_space=pltpu.SMEM)] + [pl.BlockSpec(memory_space=pltpu.HBM)] * 8,
        out_specs=[pl.BlockSpec(memory_space=pl.ANY)] * 3,
        scratch_shapes=[
            pltpu.SMEM((NBLK,), jnp.int32),
            pltpu.SMEM((1,), jnp.int32),
            pltpu.VMEM((F, OC), jnp.bfloat16),
            pltpu.VMEM((1, OC), jnp.int32),
            pltpu.VMEM((NBLK, BC, BR), jnp.bfloat16),
            pltpu.VMEM((NBLK, BC), jnp.int32),
            pltpu.VMEM((NBLK, BR), jnp.int32),
            pltpu.VMEM((AY, AX), f32),
            pltpu.VMEM((16, OC), f32),
            pltpu.VMEM((8, OC // 2), f32),
            pltpu.VMEM((384, BC), jnp.bfloat16),
            pltpu.VMEM((NBLK, 16, BR), f32),
            pltpu.VMEM((9, F * AY, AX), f32),
            pltpu.VMEM((2, 3, 48, AX), f32),
            pltpu.VMEM((3, AY, AX), f32),
            pltpu.SemaphoreType.DMA((8,)),
            pltpu.SemaphoreType.DMA((6,)),
        ],
        compiler_params=pltpu.CompilerParams(vmem_limit_bytes=60 * 1024 * 1024),
    )(side, dest, counts, ocean, land, weights, col_map, row_map, kappa)


SWEEPS = 3


def smooth_kernel(inside_ref, own_ref, top_ref, bottom_ref, out_ref, side_ref, main_ref, halo_ref):
    f32, i32 = jnp.float32, jnp.int32
    wide = 2 * AX
    tall = AY + 16
    strip = lambda ref, at: jnp.concatenate([ref[at:at + 8, :], ref[at + 8:at + 16, :]], 1)
    below = lax.rem(lax.broadcasted_iota(i32, (8, wide), 1), AY) < 8
    ends = lambda at: jnp.where(below, strip(bottom_ref, at), strip(top_ref, at))
    for slot, (west, east) in enumerate(((strip(own_ref, 13 * AY), strip(own_ref, 13 * AY + 16)),
                                         (ends(13 * 8), ends(13 * 8 + 16)))):
        block = jnp.concatenate([east, jnp.zeros((AX - 16, wide), f32), west], 0)
        side_ref[slot, 0:AX] = block[:, :AX].T
        side_ref[slot, AX:wide] = block[:, AX:].T

    rows = lax.broadcasted_iota(i32, (tall, AX), 0)
    lane = lax.broadcasted_iota(i32, (24, AX), 1)
    inside = jnp.logical_and(jnp.logical_or(rows >= 8, inside_ref[0] == 1),
                             jnp.logical_or(rows < 8 + AY, inside_ref[1] == 1))
    for f in range(F + 1):
        keep = (lambda v, lo, hi: jnp.where(inside[lo:hi], v, 0.0)) if f < F else (lambda v, lo, hi: v)
        main_ref[f, 0:8] = keep(top_ref[8 * f:8 * f + 8], 0, 8)
        main_ref[f, 8:8 + AY] = own_ref[AY * f:AY * f + AY]
        main_ref[f, 8 + AY:tall] = keep(bottom_ref[8 * f:8 * f + 8], 8 + AY, tall)
        halo_ref[f, 0:8] = keep(side_ref[1, AY * f + 8:AY * f + 16], 0, 8)
        halo_ref[f, 8:8 + AY] = side_ref[0, AY * f:AY * f + AY]
        halo_ref[f, 8 + AY:tall] = keep(side_ref[1, AY * f:AY * f + 8], 8 + AY, tall)

    def lap(ref, f, lo, n, own_rolls, other_rolls):
        at = lambda by: ref[f, lo + by:lo + by + n]
        size = lane[:n]
        turned = {by: jnp.where(size >= by if by > 0 else size < AX + by, own_rolls[by], other_rolls[by])
                  for by in (1, -1, 2, -2)}
        near = (at(-1) + at(1)) + (turned[1] + turned[-1])
        far = (at(-2) + at(2)) + (turned[2] + turned[-2])
        return 4.0 / 3.0 * near - 1.0 / 12.0 * far - 5.0 * at(0)

    for sweep in range(SWEEPS):
        last = sweep == SWEEPS - 1
        lo, n = (8, AY) if last else (4, 24)
        kappa_main, kappa_halo = main_ref[F, lo:lo + n], halo_ref[F, lo:lo + n]
        seen = inside[4:28]
        for f in range(F):
            u, v = main_ref[f, lo:lo + n], halo_ref[f, lo:lo + n]
            u_rolls = {by: pltpu.roll(u, by % AX, 1) for by in (1, -1, 2, -2)}
            v_rolls = {by: pltpu.roll(v, by % AX, 1) for by in (1, -1, 2, -2)}
            u = u + kappa_main * lap(main_ref, f, lo, n, u_rolls, v_rolls)
            if last:
                out_ref[f] = u
            else:
                v = v + kappa_halo * lap(halo_ref, f, lo, n, v_rolls, u_rolls)
                main_ref[f, lo:lo + n] = jnp.where(seen, u, 0.0)
                halo_ref[f, lo:lo + n] = jnp.where(seen, v, 0.0)


def smooth(inside, own, top, bottom):
    vm = pl.BlockSpec(memory_space=pltpu.VMEM)
    return pl.pallas_call(
        smooth_kernel,
        out_shape=jax.ShapeDtypeStruct((F, AY, AX), jnp.float32),
        in_specs=[pl.BlockSpec(memory_space=pltpu.SMEM), vm, vm, vm],
        out_specs=vm,
        scratch_shapes=[
            pltpu.VMEM((2, 2 * AX, AX), jnp.float32),
            pltpu.VMEM((F + 1, AY + 16, AX), jnp.float32),
            pltpu.VMEM((F + 1, AY + 16, AX), jnp.float32),
        ],
        compiler_params=pltpu.CompilerParams(vmem_limit_bytes=16 * 1024 * 1024),
    )(inside, own, top, bottom)


def partners(n_row, n_col):
    at = lambda r, c: (r % n_row) * n_col + c % n_col
    chip = [[at(2 * k, c), at(2 * k + 1, c)] for k in range(n_row // 2) for c in range(n_col)]
    beside = [[at(r, c), at(r, c + 1)] for r in range(n_row) for c in range(r % 2, n_col, 2)]
    bands = [[at(2 * k + 1, c), at(2 * k + 2, c)] for k in range(n_row // 2) for c in range(n_col)]
    beyond = []
    for r in range(n_row):
        for c in range(n_col):
            step = 2 if (r + c) % 2 == 0 else -2
            beyond.append((at(r, c), at(r ^ 1, c + step)))
    return chip, beside, bands, beyond


def per_device(ocean, land, weights, col_map, row_map, dest, counts, kappa):
    both = ("row", "col")
    n_row, n_col = lax.axis_size("row"), lax.axis_size("col")
    chip, beside, bands, beyond = partners(n_row, n_col)
    row, col = lax.axis_index("row"), lax.axis_index("col")
    core = row % 2
    first = core == 0
    ahead = (row + col) % 2 == 0
    side = jnp.where(ahead, 1, 0).astype(jnp.int32)
    swap = lambda value, groups, place: lax.dynamic_index_in_dim(
        lax.all_gather(value, both, axis_index_groups=groups), place, 0, keepdims=False)
    take = lambda value, place: lax.dynamic_index_in_dim(value, place, 0, keepdims=False)
    part = lambda value, start, size, dim: lax.dynamic_slice_in_dim(value, start, size, dim)

    sent, mine, mid = remap(side.reshape(1), dest.reshape(NBLK), counts.reshape(1), ocean, land.reshape(1, OC), weights, col_map, row_map, kappa)
    other = swap(sent, chip, 1 - core)
    four = lambda a, b: jnp.pad(a, ((0, 1), (0, 0), (0, 0))) + jnp.pad(b, ((1, 0), (0, 0), (0, 0)))
    total = four(jnp.where(first, mine, other), jnp.where(first, other, mine))
    far = lax.ppermute(total[:, 208:224], both, beyond)
    near = swap(total[:, 0:208], beside, side)
    strip = near[:, 192:208] + far + total[:, 224:240]
    zero = jnp.zeros_like(mid)
    placed = four(jnp.where(first, mid, zero), jnp.where(first, zero, mid))
    field = placed + jnp.pad(near[:, 0:192], ((0, 0), (0, 16), (0, 0)))
    whole = jnp.concatenate([field, strip], 1)
    mine = part(whole, 2 * core, 2, 0)
    other = swap(part(whole, 2 - 2 * core, 2, 0), chip, 1 - core)
    east = jnp.where(ahead, mine[:, 208:], other[:, 208:])
    west = jnp.where(ahead, other[:, 208:], mine[:, 208:])
    main = mine[:, :208] + other[:, :208]
    half = lambda value, start: part(value[:208].reshape(13, AY, AX), start, 8, 1).reshape(104, AX)
    edges = jnp.concatenate([west, east], 1)
    mine_main, mine_edges = take(main, 1 - core), take(edges, 1 - core)
    out_main, out_edges = take(main, core), take(edges, core)
    sent = jnp.concatenate([out_main, out_edges, half(mine_main, 8 * core), mine_edges], 0)
    got = swap(sent, bands, core)
    outer = jnp.logical_or(row == 0, row == n_row - 1)
    got = jnp.where(outer, 0.0, got)
    own = jnp.concatenate([mine_main, mine_edges], 0) + got[:240]
    outside = jnp.concatenate([half(out_main, 8 - 8 * core), out_edges], 0) + got[240:]
    within = swap(jnp.concatenate([half(own, 8 - 8 * core), own[208:]], 0), chip, 1 - core)
    top = jnp.where(first, outside, within)
    bottom = jnp.where(first, within, outside)
    inside = jnp.stack([row != 0, row != n_row - 1]).astype(jnp.int32)
    return smooth(inside, own, top, bottom)


def solution(mesh):
    placed = (
        P("row", "col", None, None),
        P("row", "col", None),
        P("row", "col", None, None, None),
        P("row", "col", None, None),
        P("row", "col", None, None),
        P("row", "col", None, None),
        P("row", "col"),
        P("row", "col"),
    )
    return jax.shard_map(
        per_device, mesh=mesh, in_specs=placed, out_specs=P(None, "row", "col"), check_vma=False
    )
```

```python
import functools

import jax
import jax.numpy as jnp
from jax import lax
from jax.experimental import pallas as pl
from jax.experimental.pallas import tpu as pltpu
from jax.sharding import PartitionSpec as P

F, AY, AX, OC, NBLK, BC, BR = 12, 16, 128, 8192, 24, 256, 128
MIX = (1, 0)
NT = (((1,), (1,)), ((), ()))


def split2(x):
    hi = x.astype(jnp.bfloat16)
    return hi, (x - hi.astype(jnp.float32)).astype(jnp.bfloat16)


def remap_kernel(side_ref, counts_in, dest_in, ocean_in, land_in, weights_in, col_in, row_in, kappa_in,
                 sent_out, kept_out, mid_out, dest_ref, counts_ref, ocean_ref, land_ref, weight_ref, col_ref, row_ref, kappa_ref,
                 fields_ref, table_ref, rows_ref, partial_ref, tiles_ref, strips_ref, extra_ref, sems, out_sems, *, ga, gb):
    f32, bf16, i32 = jnp.float32, jnp.bfloat16, jnp.int32
    pairs = ((land_in, land_ref), (ocean_in.at[0, 0], ocean_ref), (col_in.at[0, 0], col_ref), (weights_in.at[0, 0], weight_ref),
             (counts_in, counts_ref), (row_in.at[0, 0], row_ref), (dest_in, dest_ref), (kappa_in, kappa_ref))
    copies = [pltpu.make_async_copy(a, b, sems.at[i]) for i, (a, b) in enumerate(pairs)]
    for copy in copies:
        copy.start()
    tiles_ref[...] = jnp.zeros_like(tiles_ref)
    copies[0].wait()
    copies[1].wait()
    sea = land_ref[...].astype(f32)
    high = OC // 128
    fields_ref[0:8, :] = ocean_ref[0:8, :].astype(f32) * sea
    fields_ref[8:12, :] = ocean_ref[8:12, :].astype(f32) * sea
    fields_ref[12:16, :] = jnp.zeros((4, OC), f32)
    low8 = fields_ref[8:16, :]
    down8 = pltpu.roll(low8, 4, 0)
    blocks = OC // BC
    cut = lambda a, h: a[:, h * BC:(h + 1) * BC]
    upper = fields_ref[0:8, :]
    rows_ref[0:8 * blocks, :] = jnp.concatenate([cut(upper, h) for h in range(blocks)], 0).astype(bf16)
    rows_ref[8 * blocks:12 * blocks, :] = jnp.concatenate(
        [cut(low8, 2 * p) + cut(down8, 2 * p + 1) for p in range(blocks // 2)], 0).astype(bf16)
    for p in range(high // 2):
        table_ref[:, p * 128:(p + 1) * 128] = low8[:, 256 * p:256 * p + 128] + down8[:, 256 * p + 128:256 * p + 256]
    for copy in copies[2:]:
        copy.wait()
    count = counts_ref[0]
    odd = (lax.broadcasted_iota(i32, (8, 128), 0) >= 4).astype(i32)

    def finish(b, up, down):
        picked = jnp.concatenate([up, down], 0).astype(bf16)
        value = jnp.dot(picked, weight_ref[b], preferred_element_type=f32)
        partial_ref[b] = jnp.where(b < count, value, 0.0)

    cells = lax.broadcasted_iota(i32, (BC, BC), 0)
    odd2 = (lax.broadcasted_iota(i32, (8, BC), 0) >= 4).astype(i32)

    def pick_dot(b):
        col = col_ref[pl.ds(b, 1), :]
        low = jnp.bitwise_and(col, BC - 1)
        hi = jnp.right_shift(col, 8)
        onehot = (cells == low).astype(f32).astype(bf16)
        got = jnp.dot(rows_ref[...], onehot, preferred_element_type=f32)
        hi8 = jnp.broadcast_to(hi, (8, BC))
        up = jnp.zeros((8, BC), f32)
        for h in range(blocks):
            up = jnp.where(hi8 == h, got[8 * h:8 * h + 8], up)
        pair = hi8 - odd2
        down = jnp.zeros((8, BC), f32)
        for p in range(blocks // 2):
            down = jnp.where(pair == 2 * p, got[8 * (blocks + p):8 * (blocks + p) + 8], down)
        down = down + pltpu.roll(down, 4, 0)
        finish(b, up, down)

    def pick(b):
        ups, downs = [], []
        for t in range(BC // 128):
            col = jnp.broadcast_to(col_ref[pl.ds(b, 1), :][:, 128 * t:128 * t + 128], (8, 128))
            low = jnp.bitwise_and(col, 127)
            hi8 = jnp.right_shift(col, 7)
            up = jnp.zeros((8, 128), f32)
            for h in range(high):
                got = jnp.take_along_axis(fields_ref[0:8, 128 * h:128 * h + 128], low, 1)
                up = jnp.where(hi8 == h, got, up)
            pair = hi8 - odd
            down = jnp.zeros((8, 128), f32)
            for p in range(high // 2):
                got = jnp.take_along_axis(table_ref[:, 128 * p:128 * p + 128], low, 1)
                down = jnp.where(pair == 2 * p, got, down)
            ups.append(up)
            downs.append(down + pltpu.roll(down, 4, 0))
        up = jnp.concatenate(ups, 1)
        down = jnp.concatenate(downs, 1)
        finish(b, up, down)

    def groups(n, one):
        def step(i, carry):
            for j in range(n):
                (one if MIX[j % len(MIX)] else pick_dot)(i * n + j)
            return carry
        lax.fori_loop(0, NBLK // n, step, 0)

    groups(ga, pick)
    lanes = lax.broadcasted_iota(i32, (AX, BR), 0)
    rows16 = lax.broadcasted_iota(i32, (AY, BR), 0)

    def place(b):
        cell = row_ref[pl.ds(b, 1), :]
        x = jnp.bitwise_and(cell, AX - 1)
        y = jnp.right_shift(cell, 7)
        at_x = (lanes == x).astype(f32).astype(bf16)
        at_y = rows16 == y
        value = partial_ref[b]
        head = value.astype(bf16).astype(f32)
        tail = value - head
        spread = lambda v: jnp.concatenate(
            [jnp.where(at_y, v[f:f + 1, :], 0.0) for f in range(F)], 0).astype(bf16)
        left = jnp.concatenate([spread(head), spread(tail)], 1)
        right = jnp.concatenate([at_x, at_x], 1)
        return lax.dot_general(left, right, NT, preferred_element_type=f32)

    def place_group(i, carry):
        got = [place(i * gb + j) for j in range(gb)]
        for j in range(gb):
            d = dest_ref[i * gb + j]
            slot = 3 * lax.rem(d, 3) + lax.div(d, 3)
            tiles_ref[slot] = tiles_ref[slot] + got[j]
        return carry

    lax.fori_loop(0, NBLK // gb, place_group, 0)

    side = side_ref[0]
    outs = []

    def out(source, target):
        outs.append(pltpu.make_async_copy(source, target, out_sems.at[len(outs)]))
        outs[-1].start()

    main = F * AY
    out(tiles_ref.at[pl.ds(6 - 6 * side, 3)], sent_out.at[:, 0:main])
    out(tiles_ref.at[pl.ds(6 * side, 3)], kept_out.at[:, 0:main])
    out(tiles_ref.at[pl.ds(3, 3)], mid_out.at[:, 0:main])
    er = lax.broadcasted_iota(i32, (16, AX), 0)
    ec = lax.broadcasted_iota(i32, (16, AX), 1)
    edge = (ec == jnp.where(er < 8, er, er + AX - 16)).astype(f32).astype(bf16)
    edge2 = jnp.concatenate([edge, edge], 1)
    kappa = kappa_ref[...]
    extra_ref[...] = jnp.zeros_like(extra_ref)
    extra_ref[1] = kappa
    out(extra_ref, mid_out.at[:, main:main + AY])
    for band in range(3):
        for dc in range(3):
            tile = jnp.concatenate([tiles_ref[3 * dc + band], kappa if 3 * dc + band == 4 else jnp.zeros((AY, AX), f32)], 0)
            hi, lo = split2(tile)
            strip = lax.dot_general(edge2, jnp.concatenate([hi, lo], 1), NT, preferred_element_type=f32)
            first = strip[:, 0:128]
            second = jnp.concatenate([strip[:, 128:], jnp.zeros((16, 256 - 13 * AY), f32)], 1)
            west = jnp.concatenate([first[0:8], second[0:8]], 0)
            east = jnp.concatenate([first[8:16], second[8:16]], 0)
            if dc == 1:
                strips_ref[1, band, 0:16] = east
                strips_ref[0, band, 0:16] = west
            elif dc == 2:
                strips_ref[1, band, 16:32] = east
                strips_ref[1, band, 32:48] = west
            else:
                strips_ref[0, band, 16:32] = west
                strips_ref[0, band, 32:48] = east
    out(strips_ref.at[1 - side], sent_out.at[:, main:main + 48])
    out(strips_ref.at[side], kept_out.at[:, main:main + 48])
    for copy in outs:
        copy.wait()


def remap(side, dest, counts, ocean, land, weights, col_map, row_map, kappa, ga=12, gb=24):
    f32 = jnp.float32
    return pl.pallas_call(
        functools.partial(remap_kernel, ga=ga, gb=gb),
        out_shape=(jax.ShapeDtypeStruct((3, 240, 128), f32), jax.ShapeDtypeStruct((3, 240, 128), f32), jax.ShapeDtypeStruct((3, 208, 128), f32)),
        in_specs=[pl.BlockSpec(memory_space=pltpu.SMEM)] + [pl.BlockSpec(memory_space=pltpu.HBM)] * 8,
        out_specs=[pl.BlockSpec(memory_space=pl.ANY)] * 3,
        scratch_shapes=[
            pltpu.SMEM((NBLK,), jnp.int32),
            pltpu.SMEM((1,), jnp.int32),
            pltpu.VMEM((F, OC), jnp.bfloat16),
            pltpu.VMEM((1, OC), jnp.int32),
            pltpu.VMEM((NBLK, BC, BR), jnp.bfloat16),
            pltpu.VMEM((NBLK, BC), jnp.int32),
            pltpu.VMEM((NBLK, BR), jnp.int32),
            pltpu.VMEM((AY, AX), f32),
            pltpu.VMEM((16, OC), f32),
            pltpu.VMEM((8, OC // 2), f32),
            pltpu.VMEM((384, BC), jnp.bfloat16),
            pltpu.VMEM((NBLK, 16, BR), f32),
            pltpu.VMEM((9, F * AY, AX), f32),
            pltpu.VMEM((2, 3, 48, AX), f32),
            pltpu.VMEM((3, AY, AX), f32),
            pltpu.SemaphoreType.DMA((8,)),
            pltpu.SemaphoreType.DMA((6,)),
        ],
        compiler_params=pltpu.CompilerParams(vmem_limit_bytes=32 * 1024 * 1024),
    )(side, counts, *[pltpu.with_memory_space_constraint(v, pltpu.HBM) for v in (dest, ocean, land, weights, col_map, row_map, kappa)])


SWEEPS = 3


def smooth_kernel(inside_ref, own_ref, top_ref, bottom_ref, out_ref, side_ref, main_ref, halo_ref):
    f32, i32 = jnp.float32, jnp.int32
    wide = 2 * AX
    tall = AY + 16
    strip = lambda ref, at: jnp.concatenate([ref[at:at + 8, :], ref[at + 8:at + 16, :]], 1)
    below = lax.rem(lax.broadcasted_iota(i32, (8, wide), 1), AY) < 8
    ends = lambda at: jnp.where(below, strip(bottom_ref, at), strip(top_ref, at))
    for slot, (west, east) in enumerate(((strip(own_ref, 13 * AY), strip(own_ref, 13 * AY + 16)),
                                         (ends(13 * 8), ends(13 * 8 + 16)))):
        block = jnp.concatenate([east, jnp.zeros((AX - 16, wide), f32), west], 0)
        side_ref[slot, 0:AX] = block[:, :AX].T
        side_ref[slot, AX:wide] = block[:, AX:].T

    rows = lax.broadcasted_iota(i32, (tall, AX), 0)
    lane = lax.broadcasted_iota(i32, (24, AX), 1)
    inside = jnp.logical_and(jnp.logical_or(rows >= 8, inside_ref[0] == 1),
                             jnp.logical_or(rows < 8 + AY, inside_ref[1] == 1))
    for f in range(F + 1):
        keep = (lambda v, lo, hi: jnp.where(inside[lo:hi], v, 0.0)) if f < F else (lambda v, lo, hi: v)
        main_ref[f, 0:8] = keep(top_ref[8 * f:8 * f + 8], 0, 8)
        main_ref[f, 8:8 + AY] = own_ref[AY * f:AY * f + AY]
        main_ref[f, 8 + AY:tall] = keep(bottom_ref[8 * f:8 * f + 8], 8 + AY, tall)
        halo_ref[f, 0:8] = keep(side_ref[1, AY * f + 8:AY * f + 16], 0, 8)
        halo_ref[f, 8:8 + AY] = side_ref[0, AY * f:AY * f + AY]
        halo_ref[f, 8 + AY:tall] = keep(side_ref[1, AY * f:AY * f + 8], 8 + AY, tall)

    def lap(ref, f, lo, n, own_rolls, other_rolls):
        at = lambda by: ref[f, lo + by:lo + by + n]
        size = lane[:n]
        turned = {by: jnp.where(size >= by if by > 0 else size < AX + by, own_rolls[by], other_rolls[by])
                  for by in (1, -1, 2, -2)}
        near = (at(-1) + at(1)) + (turned[1] + turned[-1])
        far = (at(-2) + at(2)) + (turned[2] + turned[-2])
        return 4.0 / 3.0 * near - 1.0 / 12.0 * far - 5.0 * at(0)

    for sweep in range(SWEEPS):
        last = sweep == SWEEPS - 1
        lo, n = (8, AY) if last else (4, 24)
        kappa_main, kappa_halo = main_ref[F, lo:lo + n], halo_ref[F, lo:lo + n]
        seen = inside[4:28]
        for f in range(F):
            u, v = main_ref[f, lo:lo + n], halo_ref[f, lo:lo + n]
            u_rolls = {by: pltpu.roll(u, by % AX, 1) for by in (1, -1, 2, -2)}
            v_rolls = {by: pltpu.roll(v, by % AX, 1) for by in (1, -1, 2, -2)}
            u = u + kappa_main * lap(main_ref, f, lo, n, u_rolls, v_rolls)
            if last:
                out_ref[f] = u
            else:
                v = v + kappa_halo * lap(halo_ref, f, lo, n, v_rolls, u_rolls)
                main_ref[f, lo:lo + n] = jnp.where(seen, u, 0.0)
                halo_ref[f, lo:lo + n] = jnp.where(seen, v, 0.0)


def smooth(inside, own, top, bottom):
    vm = pl.BlockSpec(memory_space=pltpu.VMEM)
    return pl.pallas_call(
        smooth_kernel,
        out_shape=jax.ShapeDtypeStruct((F, AY, AX), jnp.float32),
        in_specs=[pl.BlockSpec(memory_space=pltpu.SMEM), vm, vm, vm],
        out_specs=vm,
        scratch_shapes=[
            pltpu.VMEM((2, 2 * AX, AX), jnp.float32),
            pltpu.VMEM((F + 1, AY + 16, AX), jnp.float32),
            pltpu.VMEM((F + 1, AY + 16, AX), jnp.float32),
        ],
        compiler_params=pltpu.CompilerParams(vmem_limit_bytes=16 * 1024 * 1024),
    )(inside, own, top, bottom)


def partners(n_row, n_col):
    at = lambda r, c: (r % n_row) * n_col + c % n_col
    chip = [[at(2 * k, c), at(2 * k + 1, c)] for k in range(n_row // 2) for c in range(n_col)]
    beside = [[at(r, c), at(r, c + 1)] for r in range(n_row) for c in range(r % 2, n_col, 2)]
    bands = [[at(2 * k + 1, c), at(2 * k + 2, c)] for k in range(n_row // 2 - 1) for c in range(n_col)]
    bands += [[at(r, c), at(r, c + 1)] for r in (0, n_row - 1) for c in range(0, n_col, 2)]
    beyond = []
    for r in range(n_row):
        for c in range(n_col):
            step = 2 if (r + c) % 2 == 0 else -2
            beyond.append((at(r, c), at(r ^ 1, c + step)))
    return chip, beside, bands, beyond


def per_device(ocean, land, weights, col_map, row_map, dest, counts, kappa):
    both = ("row", "col")
    n_row, n_col = lax.axis_size("row"), lax.axis_size("col")
    chip, beside, bands, beyond = partners(n_row, n_col)
    row, col = lax.axis_index("row"), lax.axis_index("col")
    core = row % 2
    first = core == 0
    ahead = (row + col) % 2 == 0
    side = jnp.where(ahead, 1, 0).astype(jnp.int32)
    swap = lambda value, groups, place: lax.dynamic_index_in_dim(
        lax.all_gather(value, both, axis_index_groups=groups), place, 0, keepdims=False)
    take = lambda value, place: lax.dynamic_index_in_dim(value, place, 0, keepdims=False)
    part = lambda value, start, size, dim: lax.dynamic_slice_in_dim(value, start, size, dim)

    sent, mine, mid = remap(side.reshape(1), dest.reshape(NBLK), counts.reshape(1), ocean, land.reshape(1, OC), weights, col_map, row_map, kappa)
    other = swap(sent, chip, 1 - core)
    four = lambda a, b: jnp.pad(a, ((0, 1), (0, 0), (0, 0))) + jnp.pad(b, ((1, 0), (0, 0), (0, 0)))
    total = four(jnp.where(first, mine, other), jnp.where(first, other, mine))
    far = lax.ppermute(total[:, 208:224], both, beyond)
    near = swap(total[:, 0:208], beside, side)
    strip = near[:, 192:208] + far + total[:, 224:240]
    zero = jnp.zeros_like(mid)
    placed = four(jnp.where(first, mid, zero), jnp.where(first, zero, mid))
    field = placed + jnp.pad(near[:, 0:192], ((0, 0), (0, 16), (0, 0)))
    whole = jnp.concatenate([field, strip], 1)
    mine = part(whole, 2 * core, 2, 0)
    other = swap(part(whole, 2 - 2 * core, 2, 0), chip, 1 - core)
    east = jnp.where(ahead, mine[:, 208:], other[:, 208:])
    west = jnp.where(ahead, other[:, 208:], mine[:, 208:])
    main = mine[:, :208] + other[:, :208]
    half = lambda value, start: part(value[:208].reshape(13, AY, AX), start, 8, 1).reshape(104, AX)
    edges = jnp.concatenate([west, east], 1)
    mine_main, mine_edges = take(main, 1 - core), take(edges, 1 - core)
    out_main, out_edges = take(main, core), take(edges, core)
    sent = jnp.concatenate([out_main, out_edges, half(mine_main, 8 * core), mine_edges], 0)
    got = swap(sent, bands, core)
    outer = jnp.logical_or(row == 0, row == n_row - 1)
    got = jnp.where(outer, 0.0, got)
    own = jnp.concatenate([mine_main, mine_edges], 0) + got[:240]
    outside = jnp.concatenate([half(out_main, 8 - 8 * core), out_edges], 0) + got[240:]
    within = swap(jnp.concatenate([half(own, 8 - 8 * core), own[208:]], 0), chip, 1 - core)
    top = jnp.where(first, outside, within)
    bottom = jnp.where(first, within, outside)
    inside = jnp.stack([row != 0, row != n_row - 1]).astype(jnp.int32)
    return smooth(inside, own, top, bottom)


def solution(mesh):
    placed = (
        P("row", "col", None, None),
        P("row", "col", None),
        P("row", "col", None, None, None),
        P("row", "col", None, None),
        P("row", "col", None, None),
        P("row", "col", None, None),
        P("row", "col"),
        P("row", "col"),
    )
    return jax.shard_map(
        per_device, mesh=mesh, in_specs=placed, out_specs=P(None, "row", "col"), check_vma=False
    )
```

```python
import functools

import jax
import jax.numpy as jnp
from jax import lax
from jax.experimental import pallas as pl
from jax.experimental.pallas import tpu as pltpu
from jax.sharding import PartitionSpec as P

F, AY, AX, OC, NBLK, BC, BR = 12, 16, 128, 8192, 24, 256, 128
MIX = (1, 0)
NT = (((1,), (1,)), ((), ()))


def split2(x):
    hi = x.astype(jnp.bfloat16)
    return hi, (x - hi.astype(jnp.float32)).astype(jnp.bfloat16)


def remap_kernel(side_ref, counts_in, dest_in, ocean_in, land_in, weights_in, col_in, row_in, kappa_in,
                 sent_out, kept_out, mid_out, dest_ref, counts_ref, ocean_ref, land_ref, weight_ref, col_ref, row_ref, kappa_ref,
                 fields_ref, table_ref, rows_ref, partial_ref, tiles_ref, raw_ref, strips_ref, extra_ref, used_ref, sems, out_sems, *, ga, gb):
    f32, bf16, i32 = jnp.float32, jnp.bfloat16, jnp.int32
    pairs = ((land_in, land_ref), (ocean_in.at[0, 0], ocean_ref), (col_in.at[0, 0], col_ref), (weights_in.at[0, 0], weight_ref),
             (counts_in, counts_ref), (row_in.at[0, 0], row_ref), (dest_in, dest_ref), (kappa_in, kappa_ref))
    copies = [pltpu.make_async_copy(a, b, sems.at[i]) for i, (a, b) in enumerate(pairs)]
    for copy in copies:
        copy.start()
    tiles_ref[...] = jnp.zeros_like(tiles_ref)
    raw_ref[...] = jnp.zeros_like(raw_ref)
    for d in range(9):
        used_ref[d] = 0
    copies[0].wait()
    copies[1].wait()
    sea = land_ref[...].astype(f32)
    high = OC // 128
    fields_ref[0:8, :] = ocean_ref[0:8, :].astype(f32) * sea
    fields_ref[8:12, :] = ocean_ref[8:12, :].astype(f32) * sea
    fields_ref[12:16, :] = jnp.zeros((4, OC), f32)
    low8 = fields_ref[8:16, :]
    down8 = pltpu.roll(low8, 4, 0)
    blocks = OC // BC
    cut = lambda a, h: a[:, h * BC:(h + 1) * BC]
    upper = fields_ref[0:8, :]
    rows_ref[0:8 * blocks, :] = jnp.concatenate([cut(upper, h) for h in range(blocks)], 0).astype(bf16)
    rows_ref[8 * blocks:12 * blocks, :] = jnp.concatenate(
        [cut(low8, 2 * p) + cut(down8, 2 * p + 1) for p in range(blocks // 2)], 0).astype(bf16)
    for p in range(high // 2):
        table_ref[:, p * 128:(p + 1) * 128] = low8[:, 256 * p:256 * p + 128] + down8[:, 256 * p + 128:256 * p + 256]
    for copy in copies[2:]:
        copy.wait()
    count = counts_ref[0]
    odd = (lax.broadcasted_iota(i32, (8, 128), 0) >= 4).astype(i32)

    def finish(b, up, down):
        picked = jnp.concatenate([up, down], 0).astype(bf16)
        value = jnp.dot(picked, weight_ref[b], preferred_element_type=f32)
        partial_ref[b] = jnp.where(b < count, value, 0.0)

    cells = lax.broadcasted_iota(i32, (BC, BC), 0)
    odd2 = (lax.broadcasted_iota(i32, (8, BC), 0) >= 4).astype(i32)

    def pick_dot(b):
        col = col_ref[pl.ds(b, 1), :]
        low = jnp.bitwise_and(col, BC - 1)
        hi = jnp.right_shift(col, 8)
        onehot = (cells == low).astype(f32).astype(bf16)
        got = jnp.dot(rows_ref[...], onehot, preferred_element_type=f32)
        hi8 = jnp.broadcast_to(hi, (8, BC))
        up = jnp.zeros((8, BC), f32)
        for h in range(blocks):
            up = jnp.where(hi8 == h, got[8 * h:8 * h + 8], up)
        pair = hi8 - odd2
        down = jnp.zeros((8, BC), f32)
        for p in range(blocks // 2):
            down = jnp.where(pair == 2 * p, got[8 * (blocks + p):8 * (blocks + p) + 8], down)
        down = down + pltpu.roll(down, 4, 0)
        finish(b, up, down)

    def pick(b):
        ups, downs = [], []
        for t in range(BC // 128):
            col = jnp.broadcast_to(col_ref[pl.ds(b, 1), :][:, 128 * t:128 * t + 128], (8, 128))
            low = jnp.bitwise_and(col, 127)
            hi8 = jnp.right_shift(col, 7)
            up = jnp.zeros((8, 128), f32)
            for h in range(high):
                got = jnp.take_along_axis(fields_ref[0:8, 128 * h:128 * h + 128], low, 1)
                up = jnp.where(hi8 == h, got, up)
            pair = hi8 - odd
            down = jnp.zeros((8, 128), f32)
            for p in range(high // 2):
                got = jnp.take_along_axis(table_ref[:, 128 * p:128 * p + 128], low, 1)
                down = jnp.where(pair == 2 * p, got, down)
            ups.append(up)
            downs.append(down + pltpu.roll(down, 4, 0))
        up = jnp.concatenate(ups, 1)
        down = jnp.concatenate(downs, 1)
        finish(b, up, down)

    def groups(n, one):
        def step(i, carry):
            for j in range(n):
                (one if MIX[j % len(MIX)] else pick_dot)(i * n + j)
            return carry
        lax.fori_loop(0, NBLK // n, step, 0)

    groups(ga, pick)
    lanes = lax.broadcasted_iota(i32, (AX, BR), 0)
    rows16 = lax.broadcasted_iota(i32, (AY, BR), 0)

    def place(b):
        cell = row_ref[pl.ds(b, 1), :]
        x = jnp.bitwise_and(cell, AX - 1)
        y = jnp.right_shift(cell, 7)
        at_x = (lanes == x).astype(f32).astype(bf16)
        at_y = rows16 == y
        value = partial_ref[b]
        head = value.astype(bf16).astype(f32)
        tail = value - head
        spread = lambda v: jnp.concatenate(
            [jnp.where(at_y, v[f:f + 1, :], 0.0) for f in range(F)], 0).astype(bf16)
        left = jnp.concatenate([spread(head), spread(tail)], 1)
        right = jnp.concatenate([at_x, at_x], 1)
        return lax.dot_general(left, right, NT, preferred_element_type=f32)

    halves = lax.broadcasted_iota(i32, (8, BR), 0) // 4

    def keep_block(b, d, dc, band):
        live = (b < count).astype(i32)
        at = used_ref[d]
        used_ref[d] = at + live
        wanted = jnp.logical_and(b < count, dc != 1)
        to = lax.div(dc, 2)
        slot = jnp.where(wanted, 4 * band + at, 12)
        raw_ref[to, jnp.where(wanted, slot, 20)] = partial_ref[b, 0:8]
        pair = jnp.where(wanted, 12 + lax.div(slot, 2), 21)
        tail = partial_ref[b, 8:16]
        raw_ref[to, pair] = jnp.where(halves == lax.rem(slot, 2), tail, raw_ref[to, pair])
        raw_ref[to, 18 + lax.div(slot, 8), pl.ds(lax.rem(slot, 8), 1), :] = row_ref[pl.ds(b, 1), :].astype(f32)

    def place_group(i, carry):
        got = [place(i * gb + j) for j in range(gb)]
        for j in range(gb):
            d = dest_ref[i * gb + j]
            dc, band = lax.rem(d, 3), lax.div(d, 3)
            tiles_ref[3 * dc + band] = tiles_ref[3 * dc + band] + got[j]
            keep_block(i * gb + j, d, dc, band)
        return carry

    lax.fori_loop(0, NBLK // gb, place_group, 0)

    side = side_ref[0]
    outs = []

    def out(source, target):
        outs.append(pltpu.make_async_copy(source, target, out_sems.at[len(outs)]))
        outs[-1].start()

    main = F * AY
    out(raw_ref.at[1 - side, pl.ds(0, 20)], sent_out.at[pl.ds(0, 20)])
    out(raw_ref.at[side, pl.ds(0, 20)], kept_out.at[pl.ds(0, 20)])
    out(tiles_ref.at[pl.ds(3, 3)], mid_out.at[:, 0:main])
    er = lax.broadcasted_iota(i32, (16, AX), 0)
    ec = lax.broadcasted_iota(i32, (16, AX), 1)
    edge = (ec == jnp.where(er < 8, er, er + AX - 16)).astype(f32).astype(bf16)
    edge2 = jnp.concatenate([edge, edge], 1)
    kappa = kappa_ref[...]
    extra_ref[...] = jnp.zeros_like(extra_ref)
    extra_ref[1] = kappa
    out(extra_ref, mid_out.at[:, main:main + AY])
    for band in range(3):
        for dc in range(3):
            tile = jnp.concatenate([tiles_ref[3 * dc + band], kappa if 3 * dc + band == 4 else jnp.zeros((AY, AX), f32)], 0)
            hi, lo = split2(tile)
            strip = lax.dot_general(edge2, jnp.concatenate([hi, lo], 1), NT, preferred_element_type=f32)
            first = strip[:, 0:128]
            second = jnp.concatenate([strip[:, 128:], jnp.zeros((16, 256 - 13 * AY), f32)], 1)
            west = (first[0:8], second[0:8])
            east = (first[8:16], second[8:16])

            def put(to, row, strip):
                strips_ref[to, 6 * band + row] = strip[0]
                strips_ref[to, 6 * band + row + 1] = strip[1]

            if dc == 1:
                put(1, 0, east)
                put(0, 0, west)
            elif dc == 2:
                put(1, 2, east)
                put(1, 4, west)
            else:
                put(0, 2, west)
                put(0, 4, east)
    out(strips_ref.at[1 - side], sent_out.at[pl.ds(20, 18)])
    out(strips_ref.at[side], kept_out.at[pl.ds(20, 18)])
    for copy in outs:
        copy.wait()


def remap(side, dest, counts, ocean, land, weights, col_map, row_map, kappa, ga=12, gb=24):
    f32 = jnp.float32
    return pl.pallas_call(
        functools.partial(remap_kernel, ga=ga, gb=gb),
        out_shape=(jax.ShapeDtypeStruct((38, 8, 128), f32), jax.ShapeDtypeStruct((38, 8, 128), f32), jax.ShapeDtypeStruct((3, 208, 128), f32)),
        in_specs=[pl.BlockSpec(memory_space=pltpu.SMEM)] + [pl.BlockSpec(memory_space=pltpu.HBM)] * 8,
        out_specs=[pl.BlockSpec(memory_space=pl.ANY)] * 3,
        scratch_shapes=[
            pltpu.SMEM((NBLK,), jnp.int32),
            pltpu.SMEM((1,), jnp.int32),
            pltpu.VMEM((F, OC), jnp.bfloat16),
            pltpu.VMEM((1, OC), jnp.int32),
            pltpu.VMEM((NBLK, BC, BR), jnp.bfloat16),
            pltpu.VMEM((NBLK, BC), jnp.int32),
            pltpu.VMEM((NBLK, BR), jnp.int32),
            pltpu.VMEM((AY, AX), f32),
            pltpu.VMEM((16, OC), f32),
            pltpu.VMEM((8, OC // 2), f32),
            pltpu.VMEM((384, BC), jnp.bfloat16),
            pltpu.VMEM((NBLK, 16, BR), f32),
            pltpu.VMEM((9, F * AY, AX), f32),
            pltpu.VMEM((2, 22, 8, BR), f32),
            pltpu.VMEM((2, 18, 8, AX), f32),
            pltpu.VMEM((3, AY, AX), f32),
            pltpu.SMEM((9,), jnp.int32),
            pltpu.SemaphoreType.DMA((8,)),
            pltpu.SemaphoreType.DMA((6,)),
        ],
        compiler_params=pltpu.CompilerParams(vmem_limit_bytes=32 * 1024 * 1024),
    )(side, counts, *[pltpu.with_memory_space_constraint(v, pltpu.HBM) for v in (dest, ocean, land, weights, col_map, row_map, kappa)])


def collect_kernel(place_ref, got_ref, mid_ref, far_ref, beside_ref, sent_ref, kept_ref, total_ref):
    f32, bf16, i32 = jnp.float32, jnp.bfloat16, jnp.int32
    core, side = place_ref[0], place_ref[1]
    main = 13 * AY
    total_ref[:, 0:main] = jnp.zeros((4, main, AX), f32)
    total_ref[pl.ds(core, 3), 0:main] = mid_ref[...]
    for q in range(4):
        for i in range(2):
            at = main + 8 * i
            total_ref[q, at:at + 8] = (got_ref[side, 40 + 2 * q + i] + far_ref[q, 8 * i:8 * i + 8]
                                       + beside_ref[q, 8 * i:8 * i + 8])
    lanes = lax.broadcasted_iota(i32, (AX, BR), 0)
    rows16 = lax.broadcasted_iota(i32, (AY, BR), 0)

    def factors(t, slot):
        base = 20 * t
        last = 4 * (slot % 2)
        value = jnp.concatenate([got_ref[side, base + slot], got_ref[side, base + 12 + slot // 2][last:last + 4]], 0)
        cell = got_ref[side, base + 18 + slot // 8][slot % 8:slot % 8 + 1].astype(i32)
        at_x = (lanes == jnp.bitwise_and(cell, AX - 1)).astype(f32).astype(bf16)
        at_y = rows16 == jnp.right_shift(cell, 7)
        head = value.astype(bf16).astype(f32)
        tail = value - head
        spread = lambda v: jnp.concatenate([jnp.where(at_y, v[f:f + 1, :], 0.0) for f in range(F)], 0).astype(bf16)
        return jnp.concatenate([spread(head), spread(tail)], 1), jnp.concatenate([at_x, at_x], 1)

    for q in range(4):
        slots = [(t, 4 * (q - t) + k) for t in range(2) if 0 <= q - t < 3 for k in range(4)]
        added = jnp.zeros((F * AY, AX), f32)
        for t, slot in slots:
            left, right = factors(t, slot)
            added = added + lax.dot_general(left, right, NT, preferred_element_type=f32)
        total_ref[q, 0:F * AY] = total_ref[q, 0:F * AY] + added
    kept_ref[...] = total_ref[pl.ds(2 * core, 2)]
    sent_ref[...] = total_ref[pl.ds(2 - 2 * core, 2)]


def collect(place, got, mid, far, beside):
    vm = pl.BlockSpec(memory_space=pltpu.VMEM)
    half = jax.ShapeDtypeStruct((2, 224, AX), jnp.float32)
    return pl.pallas_call(
        collect_kernel,
        out_shape=(half, half),
        in_specs=[pl.BlockSpec(memory_space=pltpu.SMEM), vm, vm, vm, vm],
        out_specs=(vm, vm),
        scratch_shapes=[pltpu.VMEM((4, 224, AX), jnp.float32)],
        compiler_params=pltpu.CompilerParams(vmem_limit_bytes=16 * 1024 * 1024),
    )(place, got, mid, far, beside)


SWEEPS = 3


def smooth_kernel(inside_ref, own_ref, top_ref, bottom_ref, out_ref, side_ref, main_ref, halo_ref):
    f32, i32 = jnp.float32, jnp.int32
    wide = 2 * AX
    tall = AY + 16
    strip = lambda ref, at: jnp.concatenate([ref[at:at + 8, :], ref[at + 8:at + 16, :]], 1)
    below = lax.rem(lax.broadcasted_iota(i32, (8, wide), 1), AY) < 8
    ends = lambda at: jnp.where(below, strip(bottom_ref, at), strip(top_ref, at))
    for slot, (west, east) in enumerate(((strip(own_ref, 13 * AY), strip(own_ref, 13 * AY + 16)),
                                         (ends(13 * 8), ends(13 * 8 + 16)))):
        block = jnp.concatenate([east, jnp.zeros((AX - 16, wide), f32), west], 0)
        side_ref[slot, 0:AX] = block[:, :AX].T
        side_ref[slot, AX:wide] = block[:, AX:].T

    rows = lax.broadcasted_iota(i32, (tall, AX), 0)
    lane = lax.broadcasted_iota(i32, (24, AX), 1)
    inside = jnp.logical_and(jnp.logical_or(rows >= 8, inside_ref[0] == 1),
                             jnp.logical_or(rows < 8 + AY, inside_ref[1] == 1))
    for f in range(F + 1):
        keep = (lambda v, lo, hi: jnp.where(inside[lo:hi], v, 0.0)) if f < F else (lambda v, lo, hi: v)
        main_ref[f, 0:8] = keep(top_ref[8 * f:8 * f + 8], 0, 8)
        main_ref[f, 8:8 + AY] = own_ref[AY * f:AY * f + AY]
        main_ref[f, 8 + AY:tall] = keep(bottom_ref[8 * f:8 * f + 8], 8 + AY, tall)
        halo_ref[f, 0:8] = keep(side_ref[1, AY * f + 8:AY * f + 16], 0, 8)
        halo_ref[f, 8:8 + AY] = side_ref[0, AY * f:AY * f + AY]
        halo_ref[f, 8 + AY:tall] = keep(side_ref[1, AY * f:AY * f + 8], 8 + AY, tall)

    def lap(ref, f, lo, n, own_rolls, other_rolls):
        at = lambda by: ref[f, lo + by:lo + by + n]
        size = lane[:n]
        turned = {by: jnp.where(size >= by if by > 0 else size < AX + by, own_rolls[by], other_rolls[by])
                  for by in (1, -1, 2, -2)}
        near = (at(-1) + at(1)) + (turned[1] + turned[-1])
        far = (at(-2) + at(2)) + (turned[2] + turned[-2])
        return 4.0 / 3.0 * near - 1.0 / 12.0 * far - 5.0 * at(0)

    for sweep in range(SWEEPS):
        last = sweep == SWEEPS - 1
        lo, n = (8, AY) if last else (4, 24)
        kappa_main, kappa_halo = main_ref[F, lo:lo + n], halo_ref[F, lo:lo + n]
        seen = inside[4:28]
        for f in range(F):
            u, v = main_ref[f, lo:lo + n], halo_ref[f, lo:lo + n]
            u_rolls = {by: pltpu.roll(u, by % AX, 1) for by in (1, -1, 2, -2)}
            v_rolls = {by: pltpu.roll(v, by % AX, 1) for by in (1, -1, 2, -2)}
            u = u + kappa_main * lap(main_ref, f, lo, n, u_rolls, v_rolls)
            if last:
                out_ref[f] = u
            else:
                v = v + kappa_halo * lap(halo_ref, f, lo, n, v_rolls, u_rolls)
                main_ref[f, lo:lo + n] = jnp.where(seen, u, 0.0)
                halo_ref[f, lo:lo + n] = jnp.where(seen, v, 0.0)


def smooth(inside, own, top, bottom):
    vm = pl.BlockSpec(memory_space=pltpu.VMEM)
    return pl.pallas_call(
        smooth_kernel,
        out_shape=jax.ShapeDtypeStruct((F, AY, AX), jnp.float32),
        in_specs=[pl.BlockSpec(memory_space=pltpu.SMEM), vm, vm, vm],
        out_specs=vm,
        scratch_shapes=[
            pltpu.VMEM((2, 2 * AX, AX), jnp.float32),
            pltpu.VMEM((F + 1, AY + 16, AX), jnp.float32),
            pltpu.VMEM((F + 1, AY + 16, AX), jnp.float32),
        ],
        compiler_params=pltpu.CompilerParams(vmem_limit_bytes=16 * 1024 * 1024),
    )(inside, own, top, bottom)


def partners(n_row, n_col):
    at = lambda r, c: (r % n_row) * n_col + c % n_col
    chip = [[at(2 * k, c), at(2 * k + 1, c)] for k in range(n_row // 2) for c in range(n_col)]
    beside = [[at(r, c), at(r, c + 1)] for r in range(n_row) for c in range(r % 2, n_col, 2)]
    bands = [[at(2 * k + 1, c), at(2 * k + 2, c)] for k in range(n_row // 2 - 1) for c in range(n_col)]
    bands += [[at(r, c), at(r, c + 1)] for r in (0, n_row - 1) for c in range(0, n_col, 2)]
    beyond = []
    for r in range(n_row):
        for c in range(n_col):
            step = 2 if (r + c) % 2 == 0 else -2
            beyond.append((at(r, c), at(r ^ 1, c + step)))
    return chip, beside, bands, beyond


def per_device(ocean, land, weights, col_map, row_map, dest, counts, kappa):
    both = ("row", "col")
    n_row, n_col = lax.axis_size("row"), lax.axis_size("col")
    chip, beside, bands, beyond = partners(n_row, n_col)
    row, col = lax.axis_index("row"), lax.axis_index("col")
    core = row % 2
    first = core == 0
    ahead = (row + col) % 2 == 0
    side = jnp.where(ahead, 1, 0).astype(jnp.int32)
    swap = lambda value, groups, place: lax.dynamic_index_in_dim(
        lax.all_gather(value, both, axis_index_groups=groups), place, 0, keepdims=False)
    take = lambda value, place: lax.dynamic_index_in_dim(value, place, 0, keepdims=False)
    part = lambda value, start, size, dim: lax.dynamic_slice_in_dim(value, start, size, dim)

    sent, mine, mid = remap(side.reshape(1), dest.reshape(NBLK), counts.reshape(1), ocean, land.reshape(1, OC), weights, col_map, row_map, kappa)
    other = swap(sent, chip, 1 - core)
    lower, upper = jnp.where(first, mine, other), jnp.where(first, other, mine)
    lift = lambda value, before: jnp.pad(value[20:].reshape(3, 48, AX), ((before, 1 - before), (0, 0), (0, 0)))
    strips = lift(lower, 0) + lift(upper, 1)
    far = lax.ppermute(strips[:, 16:32], both, beyond)
    near = lax.all_gather(jnp.concatenate([lower[:20], upper[:20], strips[:, 0:16].reshape(8, 8, AX)], 0),
                          both, axis_index_groups=beside)
    sent, mine = collect(jnp.stack([core, side]).astype(jnp.int32), near, mid, far, strips[:, 32:48])
    other = swap(sent, chip, 1 - core)
    east = jnp.where(ahead, mine[:, 208:], other[:, 208:])
    west = jnp.where(ahead, other[:, 208:], mine[:, 208:])
    main = mine[:, :208] + other[:, :208]
    half = lambda value, start: part(value[:208].reshape(13, AY, AX), start, 8, 1).reshape(104, AX)
    edges = jnp.concatenate([west, east], 1)
    mine_main, mine_edges = take(main, 1 - core), take(edges, 1 - core)
    out_main, out_edges = take(main, core), take(edges, core)
    sent = jnp.concatenate([out_main, out_edges, half(mine_main, 8 * core), mine_edges], 0)
    got = swap(sent, bands, core)
    outer = jnp.logical_or(row == 0, row == n_row - 1)
    got = jnp.where(outer, 0.0, got)
    own = jnp.concatenate([mine_main, mine_edges], 0) + got[:240]
    outside = jnp.concatenate([half(out_main, 8 - 8 * core), out_edges], 0) + got[240:]
    within = swap(jnp.concatenate([half(own, 8 - 8 * core), own[208:]], 0), chip, 1 - core)
    top = jnp.where(first, outside, within)
    bottom = jnp.where(first, within, outside)
    inside = jnp.stack([row != 0, row != n_row - 1]).astype(jnp.int32)
    return smooth(inside, own, top, bottom)


def solution(mesh):
    placed = (
        P("row", "col", None, None),
        P("row", "col", None),
        P("row", "col", None, None, None),
        P("row", "col", None, None),
        P("row", "col", None, None),
        P("row", "col", None, None),
        P("row", "col"),
        P("row", "col"),
    )
    return jax.shard_map(
        per_device, mesh=mesh, in_specs=placed, out_specs=P(None, "row", "col"), check_vma=False
    )
```

```python
import functools

import jax
import jax.numpy as jnp
from jax import lax
from jax.experimental import pallas as pl
from jax.experimental.pallas import tpu as pltpu
from jax.sharding import PartitionSpec as P

F, AY, AX, OC, NBLK, BC, BR = 12, 16, 128, 8192, 24, 256, 128
MIX = (0, 1)
NT = (((1,), (1,)), ((), ()))


def split2(x):
    hi = x.astype(jnp.bfloat16)
    return hi, (x - hi.astype(jnp.float32)).astype(jnp.bfloat16)


def remap_kernel(side_ref, counts_in, dest_in, ocean_in, land_in, weights_in, col_in, row_in, kappa_in,
                 sent_ref, kept_ref, mid_ref, dest_ref, counts_ref, ocean_ref, land_ref, weight_ref, col_ref, row_ref, kappa_ref,
                 fields_ref, table_ref, rows_ref, partial_ref, tiles_ref, raw_ref, strips_ref, used_ref, sems, *, ga, gb):
    f32, bf16, i32 = jnp.float32, jnp.bfloat16, jnp.int32
    pairs = ((land_in, land_ref), (ocean_in.at[0, 0], ocean_ref), (col_in.at[0, 0], col_ref), (weights_in.at[0, 0], weight_ref),
             (counts_in, counts_ref), (row_in.at[0, 0], row_ref), (dest_in, dest_ref), (kappa_in, kappa_ref))
    copies = [pltpu.make_async_copy(a, b, sems.at[i]) for i, (a, b) in enumerate(pairs)]
    for copy in copies:
        copy.start()
    tiles_ref[...] = jnp.zeros_like(tiles_ref)
    raw_ref[...] = jnp.zeros_like(raw_ref)
    for d in range(9):
        used_ref[d] = 0
    copies[0].wait()
    copies[1].wait()
    sea = land_ref[...].astype(f32)
    high = OC // 128
    fields_ref[0:8, :] = ocean_ref[0:8, :].astype(f32) * sea
    fields_ref[8:12, :] = ocean_ref[8:12, :].astype(f32) * sea
    fields_ref[12:16, :] = jnp.zeros((4, OC), f32)
    low8 = fields_ref[8:16, :]
    down8 = pltpu.roll(low8, 4, 0)
    deep = 512
    blocks = OC // deep
    cut = lambda a, h: a[:, h * deep:(h + 1) * deep]
    upper = fields_ref[0:8, :]
    rows_ref[0:8 * blocks, :] = jnp.concatenate([cut(upper, h) for h in range(blocks)], 0).astype(bf16)
    rows_ref[8 * blocks:12 * blocks, :] = jnp.concatenate(
        [cut(low8, 2 * p) + cut(down8, 2 * p + 1) for p in range(blocks // 2)], 0).astype(bf16)
    for p in range(high // 2):
        table_ref[:, p * 128:(p + 1) * 128] = low8[:, 256 * p:256 * p + 128] + down8[:, 256 * p + 128:256 * p + 256]
    for copy in copies[2:]:
        copy.wait()
    count = counts_ref[0]
    odd = (lax.broadcasted_iota(i32, (8, 128), 0) >= 4).astype(i32)

    def finish(b, up, down):
        picked = jnp.concatenate([up, down], 0).astype(bf16)
        value = jnp.dot(picked, weight_ref[b], preferred_element_type=f32)
        partial_ref[b] = jnp.where(b < count, value, 0.0)

    cells = lax.broadcasted_iota(i32, (deep, BC), 0).astype(jnp.int16)
    odd2 = (lax.broadcasted_iota(i32, (8, BC), 0) >= 4).astype(i32)

    def pick_dot(b):
        col = col_ref[pl.ds(b, 1), :]
        low = jnp.bitwise_and(col, deep - 1)
        hi = jnp.right_shift(col, 9)
        onehot = jnp.where(cells == jnp.broadcast_to(low, (deep, BC)).astype(jnp.int16), jnp.ones((), bf16), jnp.zeros((), bf16))
        got = jnp.dot(rows_ref[...], onehot, preferred_element_type=f32)
        hi8 = jnp.broadcast_to(hi, (8, BC))
        up = jnp.zeros((8, BC), f32)
        for h in range(blocks):
            up = jnp.where(hi8 == h, got[8 * h:8 * h + 8], up)
        pair = hi8 - odd2
        down = jnp.zeros((8, BC), f32)
        for p in range(blocks // 2):
            down = jnp.where(pair == 2 * p, got[8 * (blocks + p):8 * (blocks + p) + 8], down)
        down = down + pltpu.roll(down, 4, 0)
        finish(b, up, down)

    def pick(b):
        ups, downs = [], []
        for t in range(BC // 128):
            col = jnp.broadcast_to(col_ref[pl.ds(b, 1), :][:, 128 * t:128 * t + 128], (8, 128))
            low = jnp.bitwise_and(col, 127)
            hi8 = jnp.right_shift(col, 7)
            up = jnp.zeros((8, 128), f32)
            for h in range(high):
                got = jnp.take_along_axis(fields_ref[0:8, 128 * h:128 * h + 128], low, 1)
                up = jnp.where(hi8 == h, got, up)
            pair = hi8 - odd
            down = jnp.zeros((8, 128), f32)
            for p in range(high // 2):
                got = jnp.take_along_axis(table_ref[:, 128 * p:128 * p + 128], low, 1)
                down = jnp.where(pair == 2 * p, got, down)
            ups.append(up)
            downs.append(down + pltpu.roll(down, 4, 0))
        up = jnp.concatenate(ups, 1)
        down = jnp.concatenate(downs, 1)
        finish(b, up, down)

    def groups(n, one):
        def step(i, carry):
            for j in range(n):
                (one if MIX[j % len(MIX)] else pick_dot)(i * n + j)
            return carry
        lax.fori_loop(0, NBLK // n, step, 0)

    groups(ga, pick)
    lanes = lax.broadcasted_iota(i32, (AX, BR), 0)
    rows16 = lax.broadcasted_iota(i32, (AY, BR), 0)

    def place(b):
        cell = row_ref[pl.ds(b, 1), :]
        x = jnp.bitwise_and(cell, AX - 1)
        y = jnp.right_shift(cell, 7)
        at_x = (lanes == x).astype(f32).astype(bf16)
        at_y = rows16 == y
        value = partial_ref[b]
        head = value.astype(bf16).astype(f32)
        tail = value - head
        spread = lambda v: jnp.concatenate(
            [jnp.where(at_y, v[f:f + 1, :], 0.0) for f in range(F)], 0).astype(bf16)
        left = jnp.concatenate([spread(head), spread(tail)], 1)
        right = jnp.concatenate([at_x, at_x], 1)
        return lax.dot_general(left, right, NT, preferred_element_type=f32)

    halves = lax.broadcasted_iota(i32, (8, BR), 0) // 4

    def keep_block(b, d, dc, band):
        live = (b < count).astype(i32)
        at = used_ref[d]
        used_ref[d] = at + live
        wanted = jnp.logical_and(b < count, dc != 1)
        to = lax.div(dc, 2)
        slot = jnp.where(wanted, 4 * band + at, 12)
        raw_ref[to, jnp.where(wanted, slot, 20)] = partial_ref[b, 0:8]
        pair = jnp.where(wanted, 12 + lax.div(slot, 2), 21)
        tail = partial_ref[b, 8:16]
        raw_ref[to, pair] = jnp.where(halves == lax.rem(slot, 2), tail, raw_ref[to, pair])
        raw_ref[to, 18 + lax.div(slot, 8), pl.ds(lax.rem(slot, 8), 1), :] = row_ref[pl.ds(b, 1), :].astype(f32)

    def place_group(i, carry):
        got = [place(i * gb + j) for j in range(gb)]
        for j in range(gb):
            d = dest_ref[i * gb + j]
            dc, band = lax.rem(d, 3), lax.div(d, 3)
            tiles_ref[3 * dc + band] = tiles_ref[3 * dc + band] + got[j]
            keep_block(i * gb + j, d, dc, band)
        return carry

    lax.fori_loop(0, NBLK // gb, place_group, 0)

    side = side_ref[0]
    main = F * AY
    for band in range(3):
        mid_ref[band, 0:main] = tiles_ref[3 + band]
        mid_ref[band, main:main + AY] = kappa_ref[...] if band == 1 else jnp.zeros((AY, AX), f32)
    sent_ref[0:20] = raw_ref[1 - side, 0:20]
    kept_ref[0:20] = raw_ref[side, 0:20]
    er = lax.broadcasted_iota(i32, (16, AX), 0)
    ec = lax.broadcasted_iota(i32, (16, AX), 1)
    edge = (ec == jnp.where(er < 8, er, er + AX - 16)).astype(f32).astype(bf16)
    edge2 = jnp.concatenate([edge, edge], 1)
    kappa = kappa_ref[...]
    for band in range(3):
        for dc in range(3):
            tile = jnp.concatenate([tiles_ref[3 * dc + band], kappa if 3 * dc + band == 4 else jnp.zeros((AY, AX), f32)], 0)
            blank = jnp.zeros((128 - 13 * 8, AX), f32)
            tile = jnp.concatenate([tile[AY * f:AY * f + 8] for f in range(13)] + [blank]
                                   + [tile[AY * f + 8:AY * f + AY] for f in range(13)] + [blank], 0)
            hi, lo = split2(tile)
            strip = lax.dot_general(edge2, jnp.concatenate([hi, lo], 1), NT, preferred_element_type=f32)
            first, second = strip[:, 0:128], strip[:, 128:256]
            west = (first[0:8], second[0:8])
            east = (first[8:16], second[8:16])

            def put(to, row, strip):
                strips_ref[to, 6 * band + row] = strip[0]
                strips_ref[to, 6 * band + row + 1] = strip[1]

            if dc == 1:
                put(1, 0, east)
                put(0, 0, west)
            elif dc == 2:
                put(1, 2, east)
                put(1, 4, west)
            else:
                put(0, 2, west)
                put(0, 4, east)
    sent_ref[20:38] = strips_ref[1 - side]
    kept_ref[20:38] = strips_ref[side]


def remap(side, dest, counts, ocean, land, weights, col_map, row_map, kappa, ga=12, gb=24):
    f32 = jnp.float32
    return pl.pallas_call(
        functools.partial(remap_kernel, ga=ga, gb=gb),
        out_shape=(jax.ShapeDtypeStruct((38, 8, 128), f32), jax.ShapeDtypeStruct((38, 8, 128), f32), jax.ShapeDtypeStruct((3, 208, 128), f32)),
        in_specs=[pl.BlockSpec(memory_space=pltpu.SMEM)] + [pl.BlockSpec(memory_space=pltpu.HBM)] * 8,
        out_specs=[pl.BlockSpec(memory_space=pltpu.VMEM)] * 3,
        scratch_shapes=[
            pltpu.SMEM((NBLK,), jnp.int32),
            pltpu.SMEM((1,), jnp.int32),
            pltpu.VMEM((F, OC), jnp.bfloat16),
            pltpu.VMEM((1, OC), jnp.int32),
            pltpu.VMEM((NBLK, BC, BR), jnp.bfloat16),
            pltpu.VMEM((NBLK, BC), jnp.int32),
            pltpu.VMEM((NBLK, BR), jnp.int32),
            pltpu.VMEM((AY, AX), f32),
            pltpu.VMEM((16, OC), f32),
            pltpu.VMEM((8, OC // 2), f32),
            pltpu.VMEM((192, 512), jnp.bfloat16),
            pltpu.VMEM((NBLK, 16, BR), f32),
            pltpu.VMEM((9, F * AY, AX), f32),
            pltpu.VMEM((2, 22, 8, BR), f32),
            pltpu.VMEM((2, 18, 8, AX), f32),
            pltpu.SMEM((9,), jnp.int32),
            pltpu.SemaphoreType.DMA((8,)),
        ],
        compiler_params=pltpu.CompilerParams(vmem_limit_bytes=32 * 1024 * 1024),
    )(side, counts, *[pltpu.with_memory_space_constraint(v, pltpu.HBM) for v in (dest, ocean, land, weights, col_map, row_map, kappa)])


def collect_kernel(place_ref, got_ref, mid_ref, far_ref, beside_ref, sent_ref, kept_ref, total_ref):
    f32, bf16, i32 = jnp.float32, jnp.bfloat16, jnp.int32
    core, side = place_ref[0], place_ref[1]
    main = 13 * AY
    total_ref[:, 0:main] = jnp.zeros((4, main, AX), f32)
    total_ref[pl.ds(core, 3), 0:main] = mid_ref[...]
    for q in range(4):
        for i in range(2):
            at = main + 8 * i
            total_ref[q, at:at + 8] = (got_ref[side, 40 + 2 * q + i] + far_ref[q, 8 * i:8 * i + 8]
                                       + beside_ref[q, 8 * i:8 * i + 8])
    lanes = lax.broadcasted_iota(i32, (AX, BR), 0)
    rows16 = lax.broadcasted_iota(i32, (AY, BR), 0)

    def factors(t, slot):
        base = 20 * t
        last = 4 * (slot % 2)
        value = jnp.concatenate([got_ref[side, base + slot], got_ref[side, base + 12 + slot // 2][last:last + 4]], 0)
        cell = got_ref[side, base + 18 + slot // 8][slot % 8:slot % 8 + 1].astype(i32)
        at_x = (lanes == jnp.bitwise_and(cell, AX - 1)).astype(f32).astype(bf16)
        at_y = rows16 == jnp.right_shift(cell, 7)
        head = value.astype(bf16).astype(f32)
        tail = value - head
        spread = lambda v: jnp.concatenate([jnp.where(at_y, v[f:f + 1, :], 0.0) for f in range(F)], 0).astype(bf16)
        return jnp.concatenate([spread(head), spread(tail)], 1), jnp.concatenate([at_x, at_x], 1)

    for q in range(4):
        slots = [(t, 4 * (q - t) + k) for t in range(2) if 0 <= q - t < 3 for k in range(4)]
        added = jnp.zeros((F * AY, AX), f32)
        for t, slot in slots:
            left, right = factors(t, slot)
            added = added + lax.dot_general(left, right, NT, preferred_element_type=f32)
        total_ref[q, 0:F * AY] = total_ref[q, 0:F * AY] + added
    kept_ref[...] = total_ref[pl.ds(2 * core, 2)]
    sent_ref[...] = total_ref[pl.ds(2 - 2 * core, 2)]


def collect(place, got, mid, far, beside):
    vm = pl.BlockSpec(memory_space=pltpu.VMEM)
    half = jax.ShapeDtypeStruct((2, 224, AX), jnp.float32)
    return pl.pallas_call(
        collect_kernel,
        out_shape=(half, half),
        in_specs=[pl.BlockSpec(memory_space=pltpu.SMEM), vm, vm, vm, vm],
        out_specs=(vm, vm),
        scratch_shapes=[pltpu.VMEM((4, 224, AX), jnp.float32)],
        compiler_params=pltpu.CompilerParams(vmem_limit_bytes=16 * 1024 * 1024),
    )(place, got, mid, far, beside)


SWEEPS = 3


def smooth_kernel(inside_ref, own_ref, top_ref, bottom_ref, out_ref, side_ref, main_ref, halo_ref):
    f32, i32 = jnp.float32, jnp.int32
    wide = 2 * AX
    tall = AY + 16
    strip = lambda a, a_at, b, b_at: jnp.concatenate([a[a_at:a_at + 8, :], b[b_at:b_at + 8, :]], 1)
    for slot, (west, east) in enumerate((
            (strip(own_ref, 208, own_ref, 216), strip(own_ref, 224, own_ref, 232)),
            (strip(bottom_ref, 104, top_ref, 104), strip(bottom_ref, 112, top_ref, 112)))):
        block = jnp.concatenate([east, jnp.zeros((AX - 16, wide), f32), west], 0)
        side_ref[slot, 0:AX] = block[:, :AX].T
        side_ref[slot, AX:wide] = block[:, AX:].T

    rows = lax.broadcasted_iota(i32, (tall, AX), 0)
    lane = lax.broadcasted_iota(i32, (24, AX), 1)
    inside = jnp.logical_and(jnp.logical_or(rows >= 8, inside_ref[0] == 1),
                             jnp.logical_or(rows < 8 + AY, inside_ref[1] == 1))
    for f in range(F + 1):
        keep = (lambda v, lo, hi: jnp.where(inside[lo:hi], v, 0.0)) if f < F else (lambda v, lo, hi: v)
        main_ref[f, 0:8] = keep(top_ref[8 * f:8 * f + 8], 0, 8)
        main_ref[f, 8:8 + AY] = own_ref[AY * f:AY * f + AY]
        main_ref[f, 8 + AY:tall] = keep(bottom_ref[8 * f:8 * f + 8], 8 + AY, tall)
        halo_ref[f, 0:8] = keep(side_ref[1, AX + 8 * f:AX + 8 * f + 8], 0, 8)
        halo_ref[f, 8:16] = side_ref[0, 8 * f:8 * f + 8]
        halo_ref[f, 16:24] = side_ref[0, AX + 8 * f:AX + 8 * f + 8]
        halo_ref[f, 8 + AY:tall] = keep(side_ref[1, 8 * f:8 * f + 8], 8 + AY, tall)

    def lap(ref, f, lo, n, own_rolls, other_rolls):
        at = lambda by: ref[f, lo + by:lo + by + n]
        size = lane[:n]
        turned = {by: jnp.where(size >= by if by > 0 else size < AX + by, own_rolls[by], other_rolls[by])
                  for by in (1, -1, 2, -2)}
        near = (at(-1) + at(1)) + (turned[1] + turned[-1])
        far = (at(-2) + at(2)) + (turned[2] + turned[-2])
        return 4.0 / 3.0 * near - 1.0 / 12.0 * far - 5.0 * at(0)

    for sweep in range(SWEEPS):
        last = sweep == SWEEPS - 1
        lo, n = (8, AY) if last else (4, 24)
        kappa_main, kappa_halo = main_ref[F, lo:lo + n], halo_ref[F, lo:lo + n]
        seen = inside[4:28]
        for f in range(F):
            u, v = main_ref[f, lo:lo + n], halo_ref[f, lo:lo + n]
            u_rolls = {by: pltpu.roll(u, by % AX, 1) for by in (1, -1, 2, -2)}
            v_rolls = {by: pltpu.roll(v, by % AX, 1) for by in (1, -1, 2, -2)}
            u = u + kappa_main * lap(main_ref, f, lo, n, u_rolls, v_rolls)
            if last:
                out_ref[f] = u
            else:
                v = v + kappa_halo * lap(halo_ref, f, lo, n, v_rolls, u_rolls)
                main_ref[f, lo:lo + n] = jnp.where(seen, u, 0.0)
                halo_ref[f, lo:lo + n] = jnp.where(seen, v, 0.0)


def smooth(inside, own, top, bottom):
    vm = pl.BlockSpec(memory_space=pltpu.VMEM)
    return pl.pallas_call(
        smooth_kernel,
        out_shape=jax.ShapeDtypeStruct((F, AY, AX), jnp.float32),
        in_specs=[pl.BlockSpec(memory_space=pltpu.SMEM), vm, vm, vm],
        out_specs=vm,
        scratch_shapes=[
            pltpu.VMEM((2, 2 * AX, AX), jnp.float32),
            pltpu.VMEM((F + 1, AY + 16, AX), jnp.float32),
            pltpu.VMEM((F + 1, AY + 16, AX), jnp.float32),
        ],
        compiler_params=pltpu.CompilerParams(vmem_limit_bytes=16 * 1024 * 1024),
    )(inside, own, top, bottom)


def partners(n_row, n_col):
    at = lambda r, c: (r % n_row) * n_col + c % n_col
    chip = [[at(2 * k, c), at(2 * k + 1, c)] for k in range(n_row // 2) for c in range(n_col)]
    beside = [[at(r, c), at(r, c + 1)] for r in range(n_row) for c in range(r % 2, n_col, 2)]
    bands = [[at(2 * k + 1, c), at(2 * k + 2, c)] for k in range(n_row // 2 - 1) for c in range(n_col)]
    bands += [[at(r, c), at(r, c + 1)] for r in (0, n_row - 1) for c in range(0, n_col, 2)]
    beyond = []
    for r in range(n_row):
        for c in range(n_col):
            step = 2 if (r + c) % 2 == 0 else -2
            beyond.append((at(r, c), at(r ^ 1, c + step)))
    return chip, beside, bands, beyond


def per_device(ocean, land, weights, col_map, row_map, dest, counts, kappa):
    both = ("row", "col")
    n_row, n_col = lax.axis_size("row"), lax.axis_size("col")
    chip, beside, bands, beyond = partners(n_row, n_col)
    row, col = lax.axis_index("row"), lax.axis_index("col")
    core = row % 2
    first = core == 0
    ahead = (row + col) % 2 == 0
    side = jnp.where(ahead, 1, 0).astype(jnp.int32)
    swap = lambda value, groups, place: lax.dynamic_index_in_dim(
        lax.all_gather(value, both, axis_index_groups=groups), place, 0, keepdims=False)
    take = lambda value, place: lax.dynamic_index_in_dim(value, place, 0, keepdims=False)
    part = lambda value, start, size, dim: lax.dynamic_slice_in_dim(value, start, size, dim)

    sent, mine, mid = remap(side.reshape(1), dest.reshape(NBLK), counts.reshape(1), ocean, land.reshape(1, OC), weights, col_map, row_map, kappa)
    other = swap(sent, chip, 1 - core)
    lower, upper = jnp.where(first, mine, other), jnp.where(first, other, mine)
    lift = lambda value, before: jnp.pad(value[20:].reshape(3, 48, AX), ((before, 1 - before), (0, 0), (0, 0)))
    strips = lift(lower, 0) + lift(upper, 1)
    far = lax.ppermute(strips[:, 16:32], both, beyond)
    near = lax.all_gather(jnp.concatenate([lower[:20], upper[:20], strips[:, 0:16].reshape(8, 8, AX)], 0),
                          both, axis_index_groups=beside)
    sent, mine = collect(jnp.stack([core, side]).astype(jnp.int32), near, mid, far, strips[:, 32:48])
    other = swap(sent, chip, 1 - core)
    east = jnp.where(ahead, mine[:, 208:], other[:, 208:])
    west = jnp.where(ahead, other[:, 208:], mine[:, 208:])
    main = mine[:, :208] + other[:, :208]
    half = lambda value, start: part(value[:208].reshape(13, AY, AX), start, 8, 1).reshape(104, AX)
    edges = jnp.concatenate([west, east], 1)
    mine_main, mine_edges = take(main, 1 - core), take(edges, 1 - core)
    out_main, out_edges = take(main, core), take(edges, core)
    half_edges = lambda value, place: part(value.reshape(2, 2, 8, AX), place, 1, 1).reshape(16, AX)
    main = F * AY
    sent = jnp.concatenate([out_main[:main], out_edges, half(mine_main, 8 * core), half_edges(mine_edges, core)], 0)
    got = swap(sent, bands, core)
    outer = jnp.logical_or(row == 0, row == n_row - 1)
    got = jnp.where(outer, 0.0, got)
    own = jnp.concatenate([mine_main[:main] + got[:main], mine_main[main:], mine_edges + got[main:main + 32]], 0)
    outside = jnp.concatenate([half(out_main, 8 - 8 * core), half_edges(out_edges, 1 - core)], 0) + got[main + 32:]
    within = swap(jnp.concatenate([half(own, 8 - 8 * core), half_edges(own[208:], 1 - core)], 0), chip, 1 - core)
    top = jnp.where(first, outside, within)
    bottom = jnp.where(first, within, outside)
    inside = jnp.stack([row != 0, row != n_row - 1]).astype(jnp.int32)
    return smooth(inside, own, top, bottom)


def solution(mesh):
    placed = (
        P("row", "col", None, None),
        P("row", "col", None),
        P("row", "col", None, None, None),
        P("row", "col", None, None),
        P("row", "col", None, None),
        P("row", "col", None, None),
        P("row", "col"),
        P("row", "col"),
    )
    return jax.shard_map(
        per_device, mesh=mesh, in_specs=placed, out_specs=P(None, "row", "col"), check_vma=False
    )
```

```python
import functools

import jax
import jax.numpy as jnp
from jax import lax
from jax.experimental import pallas as pl
from jax.experimental.pallas import tpu as pltpu
from jax.sharding import PartitionSpec as P

F, AY, AX, OC, NBLK, BC, BR = 12, 16, 128, 8192, 24, 256, 128
NT = (((1,), (1,)), ((), ()))


def split2(x):
    hi = x.astype(jnp.bfloat16)
    return hi, (x - hi.astype(jnp.float32)).astype(jnp.bfloat16)


def remap_kernel(side_ref, counts_in, dest_in, ocean_in, land_in, weights_in, col_in, row_in, kappa_in,
                 sent_ref, kept_ref, mid_ref, dest_ref, counts_ref, ocean_ref, land_ref, weight_ref, col_ref, row_ref, kappa_ref,
                 fields_ref, table_ref, rows_ref, partial_ref, tiles_ref, raw_ref, strips_ref, used_ref, sems, *, ga, gb):
    f32, bf16, i32 = jnp.float32, jnp.bfloat16, jnp.int32
    pairs = ((land_in, land_ref), (ocean_in.at[0, 0], ocean_ref), (col_in.at[0, 0], col_ref), (weights_in.at[0, 0], weight_ref),
             (counts_in, counts_ref), (row_in.at[0, 0], row_ref), (dest_in, dest_ref), (kappa_in, kappa_ref))
    copies = [pltpu.make_async_copy(a, b, sems.at[i]) for i, (a, b) in enumerate(pairs)]
    for copy in copies:
        copy.start()
    tiles_ref[...] = jnp.zeros_like(tiles_ref)
    raw_ref[...] = jnp.zeros_like(raw_ref)
    for d in range(9):
        used_ref[d] = 0
    copies[0].wait()
    copies[1].wait()
    sea = land_ref[...].astype(f32)
    high = OC // 128
    fields_ref[0:8, :] = ocean_ref[0:8, :].astype(f32) * sea
    fields_ref[8:12, :] = ocean_ref[8:12, :].astype(f32) * sea
    fields_ref[12:16, :] = jnp.zeros((4, OC), f32)
    low8 = fields_ref[8:16, :]
    down8 = pltpu.roll(low8, 4, 0)
    deep = 512
    blocks = OC // deep
    cut = lambda a, h: a[:, h * deep:(h + 1) * deep]
    upper = fields_ref[0:8, :]
    rows_ref[0:8 * blocks, :] = jnp.concatenate([cut(upper, h) for h in range(blocks)], 0).astype(bf16)
    rows_ref[8 * blocks:12 * blocks, :] = jnp.concatenate(
        [cut(low8, 2 * p) + cut(down8, 2 * p + 1) for p in range(blocks // 2)], 0).astype(bf16)
    for p in range(high // 2):
        table_ref[:, p * 128:(p + 1) * 128] = low8[:, 256 * p:256 * p + 128] + down8[:, 256 * p + 128:256 * p + 256]
    for copy in copies[2:]:
        copy.wait()
    count = counts_ref[0]
    odd = (lax.broadcasted_iota(i32, (8, 128), 0) >= 4).astype(i32)

    def finish(b, up, down):
        picked = jnp.concatenate([up, down], 0).astype(bf16)
        value = jnp.dot(picked, weight_ref[b], preferred_element_type=f32)
        partial_ref[b] = jnp.where(b < count, value, 0.0)

    cells = lax.broadcasted_iota(i32, (deep, BC), 0).astype(jnp.int16)
    odd2 = (lax.broadcasted_iota(i32, (8, BC), 0) >= 4).astype(i32)

    def start_dot(b):
        col = col_ref[pl.ds(b, 1), :]
        low = jnp.bitwise_and(col, deep - 1)
        hi = jnp.right_shift(col, 9)
        onehot = jnp.where(cells == jnp.broadcast_to(low, (deep, BC)).astype(jnp.int16), jnp.ones((), bf16), jnp.zeros((), bf16))
        return hi, jnp.dot(rows_ref[...], onehot, preferred_element_type=f32)

    def select_dot(b, hi, got):
        hi8 = jnp.broadcast_to(hi, (8, BC))
        up = jnp.zeros((8, BC), f32)
        for h in range(blocks):
            up = jnp.where(hi8 == h, got[8 * h:8 * h + 8], up)
        pair = hi8 - odd2
        down = jnp.zeros((8, BC), f32)
        for p in range(blocks // 2):
            down = jnp.where(pair == 2 * p, got[8 * (blocks + p):8 * (blocks + p) + 8], down)
        down = down + pltpu.roll(down, 4, 0)
        finish(b, up, down)

    def pick(b):
        ups, downs = [], []
        for t in range(BC // 128):
            col = jnp.broadcast_to(col_ref[pl.ds(b, 1), :][:, 128 * t:128 * t + 128], (8, 128))
            low = jnp.bitwise_and(col, 127)
            hi8 = jnp.right_shift(col, 7)
            up = jnp.zeros((8, 128), f32)
            for h in range(high):
                got = jnp.take_along_axis(fields_ref[0:8, 128 * h:128 * h + 128], low, 1)
                up = jnp.where(hi8 == h, got, up)
            pair = hi8 - odd
            down = jnp.zeros((8, 128), f32)
            for p in range(high // 2):
                got = jnp.take_along_axis(table_ref[:, 128 * p:128 * p + 128], low, 1)
                down = jnp.where(pair == 2 * p, got, down)
            ups.append(up)
            downs.append(down + pltpu.roll(down, 4, 0))
        up = jnp.concatenate(ups, 1)
        down = jnp.concatenate(downs, 1)
        finish(b, up, down)

    def groups(n, one):
        def step(i, carry):
            begun = [start_dot(i * n), start_dot(i * n + 2)]
            for j in range(0, n, 2):
                one(i * n + j + 1)
                if j + 4 < n:
                    begun.append(start_dot(i * n + j + 4))
                select_dot(i * n + j, *begun.pop(0))
            return carry
        lax.fori_loop(0, NBLK // n, step, 0)

    groups(ga, pick)
    lanes = lax.broadcasted_iota(i32, (AX, BR), 0)
    rows16 = lax.broadcasted_iota(i32, (AY, BR), 0)

    def place(b):
        cell = row_ref[pl.ds(b, 1), :]
        x = jnp.bitwise_and(cell, AX - 1)
        y = jnp.right_shift(cell, 7)
        at_x = (lanes == x).astype(f32).astype(bf16)
        at_y = rows16 == y
        value = partial_ref[b]
        head = value.astype(bf16).astype(f32)
        tail = value - head
        spread = lambda v: jnp.concatenate(
            [jnp.where(at_y, v[f:f + 1, :], 0.0) for f in range(F)], 0).astype(bf16)
        left = jnp.concatenate([spread(head), spread(tail)], 1)
        right = jnp.concatenate([at_x, at_x], 1)
        return lax.dot_general(left, right, NT, preferred_element_type=f32)

    halves = lax.broadcasted_iota(i32, (8, BR), 0) // 4

    def keep_block(b, d, dc, band):
        live = (b < count).astype(i32)
        at = used_ref[d]
        used_ref[d] = at + live
        wanted = jnp.logical_and(b < count, dc != 1)
        to = lax.div(dc, 2)
        slot = jnp.where(wanted, 4 * band + at, 12)
        raw_ref[to, jnp.where(wanted, slot, 20)] = partial_ref[b, 0:8]
        pair = jnp.where(wanted, 12 + lax.div(slot, 2), 21)
        tail = partial_ref[b, 8:16]
        raw_ref[to, pair] = jnp.where(halves == lax.rem(slot, 2), tail, raw_ref[to, pair])
        raw_ref[to, 18 + lax.div(slot, 8), pl.ds(lax.rem(slot, 8), 1), :] = row_ref[pl.ds(b, 1), :].astype(f32)

    def place_group(i, carry):
        got = [place(i * gb + j) for j in range(gb)]
        for j in range(gb):
            d = dest_ref[i * gb + j]
            dc, band = lax.rem(d, 3), lax.div(d, 3)
            tiles_ref[3 * dc + band] = tiles_ref[3 * dc + band] + got[j]
            keep_block(i * gb + j, d, dc, band)
        return carry

    lax.fori_loop(0, NBLK // gb, place_group, 0)

    side = side_ref[0]
    main = F * AY
    for band in range(3):
        mid_ref[band, 0:main] = tiles_ref[3 + band]
        mid_ref[band, main:main + AY] = kappa_ref[...] if band == 1 else jnp.zeros((AY, AX), f32)
    sent_ref[0:20] = raw_ref[1 - side, 0:20]
    kept_ref[0:20] = raw_ref[side, 0:20]
    er = lax.broadcasted_iota(i32, (16, AX), 0)
    ec = lax.broadcasted_iota(i32, (16, AX), 1)
    edge = (ec == jnp.where(er < 8, er, er + AX - 16)).astype(f32).astype(bf16)
    edge2 = jnp.concatenate([edge, edge], 1)
    kappa = kappa_ref[...]
    for band in range(3):
        for dc in range(3):
            tile = jnp.concatenate([tiles_ref[3 * dc + band], kappa if 3 * dc + band == 4 else jnp.zeros((AY, AX), f32)], 0)
            blank = jnp.zeros((128 - 13 * 8, AX), f32)
            tile = jnp.concatenate([tile[AY * f:AY * f + 8] for f in range(13)] + [blank]
                                   + [tile[AY * f + 8:AY * f + AY] for f in range(13)] + [blank], 0)
            hi, lo = split2(tile)
            strip = lax.dot_general(edge2, jnp.concatenate([hi, lo], 1), NT, preferred_element_type=f32)
            first, second = strip[:, 0:128], strip[:, 128:256]
            west = (first[0:8], second[0:8])
            east = (first[8:16], second[8:16])

            def put(to, row, strip):
                strips_ref[to, 6 * band + row] = strip[0]
                strips_ref[to, 6 * band + row + 1] = strip[1]

            if dc == 1:
                put(1, 0, east)
                put(0, 0, west)
            elif dc == 2:
                put(1, 2, east)
                put(1, 4, west)
            else:
                put(0, 2, west)
                put(0, 4, east)
    sent_ref[20:38] = strips_ref[1 - side]
    kept_ref[20:38] = strips_ref[side]


def remap(side, dest, counts, ocean, land, weights, col_map, row_map, kappa, ga=12, gb=24):
    f32 = jnp.float32
    return pl.pallas_call(
        functools.partial(remap_kernel, ga=ga, gb=gb),
        out_shape=(jax.ShapeDtypeStruct((38, 8, 128), f32), jax.ShapeDtypeStruct((38, 8, 128), f32), jax.ShapeDtypeStruct((3, 208, 128), f32)),
        in_specs=[pl.BlockSpec(memory_space=pltpu.SMEM)] + [pl.BlockSpec(memory_space=pltpu.HBM)] * 8,
        out_specs=[pl.BlockSpec(memory_space=pltpu.VMEM)] * 3,
        scratch_shapes=[
            pltpu.SMEM((NBLK,), jnp.int32),
            pltpu.SMEM((1,), jnp.int32),
            pltpu.VMEM((F, OC), jnp.bfloat16),
            pltpu.VMEM((1, OC), jnp.int32),
            pltpu.VMEM((NBLK, BC, BR), jnp.bfloat16),
            pltpu.VMEM((NBLK, BC), jnp.int32),
            pltpu.VMEM((NBLK, BR), jnp.int32),
            pltpu.VMEM((AY, AX), f32),
            pltpu.VMEM((16, OC), f32),
            pltpu.VMEM((8, OC // 2), f32),
            pltpu.VMEM((192, 512), jnp.bfloat16),
            pltpu.VMEM((NBLK, 16, BR), f32),
            pltpu.VMEM((9, F * AY, AX), f32),
            pltpu.VMEM((2, 22, 8, BR), f32),
            pltpu.VMEM((2, 18, 8, AX), f32),
            pltpu.SMEM((9,), jnp.int32),
            pltpu.SemaphoreType.DMA((8,)),
        ],
        compiler_params=pltpu.CompilerParams(vmem_limit_bytes=32 * 1024 * 1024),
    )(side, counts, *[pltpu.with_memory_space_constraint(v, pltpu.HBM) for v in (dest, ocean, land, weights, col_map, row_map, kappa)])


def collect_kernel(place_ref, got_ref, mid_ref, far_ref, beside_ref, sent_ref, kept_ref, total_ref):
    f32, bf16, i32 = jnp.float32, jnp.bfloat16, jnp.int32
    core, side = place_ref[0], place_ref[1]
    main = 13 * AY
    total_ref[:, 0:main] = jnp.zeros((4, main, AX), f32)
    total_ref[pl.ds(core, 3), 0:main] = mid_ref[...]
    for q in range(4):
        for i in range(2):
            at = main + 8 * i
            total_ref[q, at:at + 8] = (got_ref[side, 40 + 2 * q + i] + far_ref[q, 8 * i:8 * i + 8]
                                       + beside_ref[q, 8 * i:8 * i + 8])
    lanes = lax.broadcasted_iota(i32, (AX, BR), 0)
    rows16 = lax.broadcasted_iota(i32, (AY, BR), 0)

    def factors(t, slot):
        base = 20 * t
        last = 4 * (slot % 2)
        value = jnp.concatenate([got_ref[side, base + slot], got_ref[side, base + 12 + slot // 2][last:last + 4]], 0)
        cell = got_ref[side, base + 18 + slot // 8][slot % 8:slot % 8 + 1].astype(i32)
        at_x = (lanes == jnp.bitwise_and(cell, AX - 1)).astype(f32).astype(bf16)
        at_y = rows16 == jnp.right_shift(cell, 7)
        head = value.astype(bf16).astype(f32)
        tail = value - head
        spread = lambda v: jnp.concatenate([jnp.where(at_y, v[f:f + 1, :], 0.0) for f in range(F)], 0).astype(bf16)
        return jnp.concatenate([spread(head), spread(tail)], 1), jnp.concatenate([at_x, at_x], 1)

    for q in range(4):
        slots = [(t, 4 * (q - t) + k) for t in range(2) if 0 <= q - t < 3 for k in range(4)]
        added = jnp.zeros((F * AY, AX), f32)
        for t, slot in slots:
            left, right = factors(t, slot)
            added = added + lax.dot_general(left, right, NT, preferred_element_type=f32)
        total_ref[q, 0:F * AY] = total_ref[q, 0:F * AY] + added
    kept_ref[...] = total_ref[pl.ds(2 * core, 2)]
    sent_ref[...] = total_ref[pl.ds(2 - 2 * core, 2)]


def collect(place, got, mid, far, beside):
    vm = pl.BlockSpec(memory_space=pltpu.VMEM)
    half = jax.ShapeDtypeStruct((2, 224, AX), jnp.float32)
    return pl.pallas_call(
        collect_kernel,
        out_shape=(half, half),
        in_specs=[pl.BlockSpec(memory_space=pltpu.SMEM), vm, vm, vm, vm],
        out_specs=(vm, vm),
        scratch_shapes=[pltpu.VMEM((4, 224, AX), jnp.float32)],
        compiler_params=pltpu.CompilerParams(vmem_limit_bytes=16 * 1024 * 1024),
    )(place, got, mid, far, beside)


SWEEPS = 3


def smooth_kernel(inside_ref, own_ref, top_ref, bottom_ref, out_ref, side_ref, main_ref, halo_ref):
    f32, i32 = jnp.float32, jnp.int32
    wide = 2 * AX
    tall = AY + 16
    strip = lambda a, a_at, b, b_at: jnp.concatenate([a[a_at:a_at + 8, :], b[b_at:b_at + 8, :]], 1)
    for slot, (west, east) in enumerate((
            (strip(own_ref, 208, own_ref, 216), strip(own_ref, 224, own_ref, 232)),
            (strip(bottom_ref, 104, top_ref, 104), strip(bottom_ref, 112, top_ref, 112)))):
        block = jnp.concatenate([east, jnp.zeros((AX - 16, wide), f32), west], 0)
        side_ref[slot, 0:AX] = block[:, :AX].T
        side_ref[slot, AX:wide] = block[:, AX:].T

    rows = lax.broadcasted_iota(i32, (tall, AX), 0)
    lane = lax.broadcasted_iota(i32, (24, AX), 1)
    inside = jnp.logical_and(jnp.logical_or(rows >= 8, inside_ref[0] == 1),
                             jnp.logical_or(rows < 8 + AY, inside_ref[1] == 1))
    for f in range(F + 1):
        keep = (lambda v, lo, hi: jnp.where(inside[lo:hi], v, 0.0)) if f < F else (lambda v, lo, hi: v)
        main_ref[f, 0:8] = keep(top_ref[8 * f:8 * f + 8], 0, 8)
        main_ref[f, 8:8 + AY] = own_ref[AY * f:AY * f + AY]
        main_ref[f, 8 + AY:tall] = keep(bottom_ref[8 * f:8 * f + 8], 8 + AY, tall)
        halo_ref[f, 0:8] = keep(side_ref[1, AX + 8 * f:AX + 8 * f + 8], 0, 8)
        halo_ref[f, 8:16] = side_ref[0, 8 * f:8 * f + 8]
        halo_ref[f, 16:24] = side_ref[0, AX + 8 * f:AX + 8 * f + 8]
        halo_ref[f, 8 + AY:tall] = keep(side_ref[1, 8 * f:8 * f + 8], 8 + AY, tall)

    def lap(ref, f, lo, n, own_rolls, other_rolls):
        at = lambda by: ref[f, lo + by:lo + by + n]
        size = lane[:n]
        turned = {by: jnp.where(size >= by if by > 0 else size < AX + by, own_rolls[by], other_rolls[by])
                  for by in (1, -1, 2, -2)}
        near = (at(-1) + at(1)) + (turned[1] + turned[-1])
        far = (at(-2) + at(2)) + (turned[2] + turned[-2])
        return 4.0 / 3.0 * near - 1.0 / 12.0 * far - 5.0 * at(0)

    for sweep in range(SWEEPS):
        last = sweep == SWEEPS - 1
        lo, n = (8, AY) if last else (4, 24)
        kappa_main, kappa_halo = main_ref[F, lo:lo + n], halo_ref[F, lo:lo + n]
        seen = inside[4:28]
        for f in range(F):
            u, v = main_ref[f, lo:lo + n], halo_ref[f, lo:lo + n]
            u_rolls = {by: pltpu.roll(u, by % AX, 1) for by in (1, -1, 2, -2)}
            v_rolls = {by: pltpu.roll(v, by % AX, 1) for by in (1, -1, 2, -2)}
            u = u + kappa_main * lap(main_ref, f, lo, n, u_rolls, v_rolls)
            if last:
                out_ref[f] = u
            else:
                v = v + kappa_halo * lap(halo_ref, f, lo, n, v_rolls, u_rolls)
                main_ref[f, lo:lo + n] = jnp.where(seen, u, 0.0)
                halo_ref[f, lo:lo + n] = jnp.where(seen, v, 0.0)


def smooth(inside, own, top, bottom):
    vm = pl.BlockSpec(memory_space=pltpu.VMEM)
    return pl.pallas_call(
        smooth_kernel,
        out_shape=jax.ShapeDtypeStruct((F, AY, AX), jnp.float32),
        in_specs=[pl.BlockSpec(memory_space=pltpu.SMEM), vm, vm, vm],
        out_specs=vm,
        scratch_shapes=[
            pltpu.VMEM((2, 2 * AX, AX), jnp.float32),
            pltpu.VMEM((F + 1, AY + 16, AX), jnp.float32),
            pltpu.VMEM((F + 1, AY + 16, AX), jnp.float32),
        ],
        compiler_params=pltpu.CompilerParams(vmem_limit_bytes=16 * 1024 * 1024),
    )(inside, own, top, bottom)


def partners(n_row, n_col):
    at = lambda r, c: (r % n_row) * n_col + c % n_col
    chip = [[at(2 * k, c), at(2 * k + 1, c)] for k in range(n_row // 2) for c in range(n_col)]
    beside = [[at(r, c), at(r, c + 1)] for r in range(n_row) for c in range(r % 2, n_col, 2)]
    bands = [[at(2 * k + 1, c), at(2 * k + 2, c)] for k in range(n_row // 2 - 1) for c in range(n_col)]
    bands += [[at(r, c), at(r, c + 1)] for r in (0, n_row - 1) for c in range(0, n_col, 2)]
    beyond = []
    for r in range(n_row):
        for c in range(n_col):
            step = 2 if (r + c) % 2 == 0 else -2
            beyond.append((at(r, c), at(r ^ 1, c + step)))
    return chip, beside, bands, beyond


def per_device(ocean, land, weights, col_map, row_map, dest, counts, kappa):
    both = ("row", "col")
    n_row, n_col = lax.axis_size("row"), lax.axis_size("col")
    chip, beside, bands, beyond = partners(n_row, n_col)
    row, col = lax.axis_index("row"), lax.axis_index("col")
    core = row % 2
    first = core == 0
    ahead = (row + col) % 2 == 0
    side = jnp.where(ahead, 1, 0).astype(jnp.int32)
    swap = lambda value, groups, place: lax.dynamic_index_in_dim(
        lax.all_gather(value, both, axis_index_groups=groups), place, 0, keepdims=False)
    take = lambda value, place: lax.dynamic_index_in_dim(value, place, 0, keepdims=False)
    part = lambda value, start, size, dim: lax.dynamic_slice_in_dim(value, start, size, dim)

    sent, mine, mid = remap(side.reshape(1), dest.reshape(NBLK), counts.reshape(1), ocean, land.reshape(1, OC), weights, col_map, row_map, kappa)
    other = swap(sent, chip, 1 - core)
    lower, upper = jnp.where(first, mine, other), jnp.where(first, other, mine)
    lift = lambda value, before: jnp.pad(value[20:].reshape(3, 48, AX), ((before, 1 - before), (0, 0), (0, 0)))
    strips = lift(lower, 0) + lift(upper, 1)
    far = lax.ppermute(strips[:, 16:32], both, beyond)
    near = lax.all_gather(jnp.concatenate([lower[:20], upper[:20], strips[:, 0:16].reshape(8, 8, AX)], 0),
                          both, axis_index_groups=beside)
    sent, mine = collect(jnp.stack([core, side]).astype(jnp.int32), near, mid, far, strips[:, 32:48])
    other = swap(sent, chip, 1 - core)
    east = jnp.where(ahead, mine[:, 208:], other[:, 208:])
    west = jnp.where(ahead, other[:, 208:], mine[:, 208:])
    main = mine[:, :208] + other[:, :208]
    half = lambda value, start: part(value[:208].reshape(13, AY, AX), start, 8, 1).reshape(104, AX)
    edges = jnp.concatenate([west, east], 1)
    mine_main, mine_edges = take(main, 1 - core), take(edges, 1 - core)
    out_main, out_edges = take(main, core), take(edges, core)
    half_edges = lambda value, place: part(value.reshape(2, 2, 8, AX), place, 1, 1).reshape(16, AX)
    main = F * AY
    sent = jnp.concatenate([out_main[:main], out_edges, half(mine_main, 8 * core), half_edges(mine_edges, core)], 0)
    got = swap(sent, bands, core)
    outer = jnp.logical_or(row == 0, row == n_row - 1)
    got = jnp.where(outer, 0.0, got)
    own = jnp.concatenate([mine_main[:main] + got[:main], mine_main[main:], mine_edges + got[main:main + 32]], 0)
    outside = jnp.concatenate([half(out_main, 8 - 8 * core), half_edges(out_edges, 1 - core)], 0) + got[main + 32:]
    within = swap(jnp.concatenate([half(own, 8 - 8 * core), half_edges(own[208:], 1 - core)], 0), chip, 1 - core)
    top = jnp.where(first, outside, within)
    bottom = jnp.where(first, within, outside)
    inside = jnp.stack([row != 0, row != n_row - 1]).astype(jnp.int32)
    return smooth(inside, own, top, bottom)


def solution(mesh):
    placed = (
        P("row", "col", None, None),
        P("row", "col", None),
        P("row", "col", None, None, None),
        P("row", "col", None, None),
        P("row", "col", None, None),
        P("row", "col", None, None),
        P("row", "col"),
        P("row", "col"),
    )
    return jax.shard_map(
        per_device, mesh=mesh, in_specs=placed, out_specs=P(None, "row", "col"), check_vma=False
    )
```

```python
import functools

import jax
import jax.numpy as jnp
from jax import lax
from jax.experimental import pallas as pl
from jax.experimental.pallas import tpu as pltpu
from jax.sharding import PartitionSpec as P

F, AY, AX, OC, NBLK, BC, BR = 12, 16, 128, 8192, 24, 256, 128
NT = (((1,), (1,)), ((), ()))


def split2(x):
    hi = x.astype(jnp.bfloat16)
    return hi, (x - hi.astype(jnp.float32)).astype(jnp.bfloat16)


def remap_kernel(side_ref, counts_in, dest_in, ocean_in, land_in, weights_in, col_in, row_in, kappa_in,
                 sent_ref, kept_ref, mid_ref, dest_ref, counts_ref, ocean_ref, land_ref, weight_ref, col_ref, row_ref, kappa_ref,
                 fields_ref, table_ref, rows_ref, partial_ref, tiles_ref, raw_ref, strips_ref, used_ref, sems, *, ga, gb):
    f32, bf16, i32 = jnp.float32, jnp.bfloat16, jnp.int32
    pairs = ((land_in, land_ref), (ocean_in.at[0, 0], ocean_ref), (col_in.at[0, 0], col_ref), (weights_in.at[0, 0], weight_ref),
             (counts_in, counts_ref), (row_in.at[0, 0], row_ref), (dest_in, dest_ref), (kappa_in, kappa_ref))
    copies = [pltpu.make_async_copy(a, b, sems.at[i]) for i, (a, b) in enumerate(pairs)]
    for copy in copies:
        copy.start()
    tiles_ref[...] = jnp.zeros_like(tiles_ref)
    raw_ref[...] = jnp.zeros_like(raw_ref)
    for d in range(9):
        used_ref[d] = 0
    copies[0].wait()
    copies[1].wait()
    sea = land_ref[...].astype(f32)
    high = OC // 128
    fields_ref[0:8, :] = ocean_ref[0:8, :].astype(f32) * sea
    fields_ref[8:12, :] = ocean_ref[8:12, :].astype(f32) * sea
    fields_ref[12:16, :] = jnp.zeros((4, OC), f32)
    low8 = fields_ref[8:16, :]
    down8 = pltpu.roll(low8, 4, 0)
    deep = 512
    blocks = OC // deep
    cut = lambda a, h: a[:, h * deep:(h + 1) * deep]
    upper = fields_ref[0:8, :]
    rows_ref[0:8 * blocks, :] = jnp.concatenate([cut(upper, h) for h in range(blocks)], 0).astype(bf16)
    rows_ref[8 * blocks:12 * blocks, :] = jnp.concatenate(
        [cut(low8, 2 * p) + cut(down8, 2 * p + 1) for p in range(blocks // 2)], 0).astype(bf16)
    for p in range(high // 2):
        table_ref[:, p * 128:(p + 1) * 128] = low8[:, 256 * p:256 * p + 128] + down8[:, 256 * p + 128:256 * p + 256]
    for copy in copies[2:]:
        copy.wait()
    count = counts_ref[0]
    odd = (lax.broadcasted_iota(i32, (8, 128), 0) >= 4).astype(i32)

    def finish(b, up, down):
        picked = jnp.concatenate([up, down], 0).astype(bf16)
        value = jnp.dot(picked, weight_ref[b], preferred_element_type=f32)
        partial_ref[b] = jnp.where(b < count, value, 0.0)

    cells = lax.broadcasted_iota(i32, (deep, BC), 0).astype(jnp.int16)
    odd2 = (lax.broadcasted_iota(i32, (8, BC), 0) >= 4).astype(i32)

    def start_dot(b):
        col = col_ref[pl.ds(b, 1), :]
        low = jnp.bitwise_and(col, deep - 1)
        hi = jnp.right_shift(col, 9)
        onehot = jnp.where(cells == jnp.broadcast_to(low, (deep, BC)).astype(jnp.int16), jnp.ones((), bf16), jnp.zeros((), bf16))
        return hi, jnp.dot(rows_ref[...], onehot, preferred_element_type=f32)

    def select_dot(b, hi, got):
        hi8 = jnp.broadcast_to(hi, (8, BC))
        up = jnp.zeros((8, BC), f32)
        for h in range(blocks):
            up = jnp.where(hi8 == h, got[8 * h:8 * h + 8], up)
        pair = hi8 - odd2
        down = jnp.zeros((8, BC), f32)
        for p in range(blocks // 2):
            down = jnp.where(pair == 2 * p, got[8 * (blocks + p):8 * (blocks + p) + 8], down)
        down = down + pltpu.roll(down, 4, 0)
        finish(b, up, down)

    def pick(b):
        ups, downs = [], []
        for t in range(BC // 128):
            col = jnp.broadcast_to(col_ref[pl.ds(b, 1), :][:, 128 * t:128 * t + 128], (8, 128))
            low = jnp.bitwise_and(col, 127)
            hi8 = jnp.right_shift(col, 7)
            up = jnp.zeros((8, 128), f32)
            for h in range(high):
                got = jnp.take_along_axis(fields_ref[0:8, 128 * h:128 * h + 128], low, 1)
                up = jnp.where(hi8 == h, got, up)
            pair = hi8 - odd
            down = jnp.zeros((8, 128), f32)
            for p in range(high // 2):
                got = jnp.take_along_axis(table_ref[:, 128 * p:128 * p + 128], low, 1)
                down = jnp.where(pair == 2 * p, got, down)
            ups.append(up)
            downs.append(down + pltpu.roll(down, 4, 0))
        up = jnp.concatenate(ups, 1)
        down = jnp.concatenate(downs, 1)
        finish(b, up, down)

    def groups(n, one):
        def step(i, carry):
            begun = [start_dot(i * n), start_dot(i * n + 2)]
            for j in range(0, n, 2):
                one(i * n + j + 1)
                if j + 4 < n:
                    begun.append(start_dot(i * n + j + 4))
                select_dot(i * n + j, *begun.pop(0))
            return carry
        lax.fori_loop(0, NBLK // n, step, 0)

    groups(ga, pick)
    lanes = lax.broadcasted_iota(i32, (AX, BR), 0)
    rows16 = lax.broadcasted_iota(i32, (AY, BR), 0)

    def place(b):
        cell = row_ref[pl.ds(b, 1), :]
        x = jnp.bitwise_and(cell, AX - 1)
        y = jnp.right_shift(cell, 7)
        at_x = (lanes == x).astype(f32).astype(bf16)
        at_y = rows16 == y
        value = partial_ref[b]
        head = value.astype(bf16).astype(f32)
        tail = value - head
        spread = lambda v: jnp.concatenate(
            [jnp.where(at_y, v[f:f + 1, :], 0.0) for f in range(F)], 0).astype(bf16)
        left = jnp.concatenate([spread(head), spread(tail)], 1)
        right = jnp.concatenate([at_x, at_x], 1)
        return lax.dot_general(left, right, NT, preferred_element_type=f32)

    halves = lax.broadcasted_iota(i32, (8, BR), 0) // 4

    def keep_block(b, d, dc, band):
        live = (b < count).astype(i32)
        at = used_ref[d]
        used_ref[d] = at + live
        wanted = jnp.logical_and(b < count, dc != 1)
        to = lax.div(dc, 2)
        slot = jnp.where(wanted, 4 * band + at, 12)
        raw_ref[to, jnp.where(wanted, slot, 20)] = partial_ref[b, 0:8]
        pair = jnp.where(wanted, 12 + lax.div(slot, 2), 21)
        tail = partial_ref[b, 8:16]
        raw_ref[to, pair] = jnp.where(halves == lax.rem(slot, 2), tail, raw_ref[to, pair])
        raw_ref[to, 18 + lax.div(slot, 8), pl.ds(lax.rem(slot, 8), 1), :] = row_ref[pl.ds(b, 1), :].astype(f32)

    def place_group(i, carry):
        got = [place(i * gb + j) for j in range(gb)]
        for j in range(gb):
            d = dest_ref[i * gb + j]
            dc, band = lax.rem(d, 3), lax.div(d, 3)
            tiles_ref[3 * dc + band] = tiles_ref[3 * dc + band] + got[j]
            keep_block(i * gb + j, d, dc, band)
        return carry

    lax.fori_loop(0, NBLK // gb, place_group, 0)

    side = side_ref[1]
    main = F * AY
    for band in range(3):
        mid_ref[band, 0:main] = tiles_ref[3 + band]
        mid_ref[band, main:main + AY] = kappa_ref[...] if band == 1 else jnp.zeros((AY, AX), f32)
    sent_ref[0:20] = raw_ref[1 - side, 0:20]
    kept_ref[0:20] = raw_ref[side, 0:20]
    er = lax.broadcasted_iota(i32, (16, AX), 0)
    ec = lax.broadcasted_iota(i32, (16, AX), 1)
    edge = (ec == jnp.where(er < 8, er, er + AX - 16)).astype(f32).astype(bf16)
    edge2 = jnp.concatenate([edge, edge], 1)
    kappa = kappa_ref[...]
    for band in range(3):
        for dc in range(3):
            tile = jnp.concatenate([tiles_ref[3 * dc + band], kappa if 3 * dc + band == 4 else jnp.zeros((AY, AX), f32)], 0)
            blank = jnp.zeros((128 - 13 * 8, AX), f32)
            tile = jnp.concatenate([tile[AY * f:AY * f + 8] for f in range(13)] + [blank]
                                   + [tile[AY * f + 8:AY * f + AY] for f in range(13)] + [blank], 0)
            hi, lo = split2(tile)
            strip = lax.dot_general(edge2, jnp.concatenate([hi, lo], 1), NT, preferred_element_type=f32)
            first, second = strip[:, 0:128], strip[:, 128:256]
            west = (first[0:8], second[0:8])
            east = (first[8:16], second[8:16])

            def put(to, row, strip):
                strips_ref[to, 6 * band + row] = strip[0]
                strips_ref[to, 6 * band + row + 1] = strip[1]

            if dc == 1:
                put(1, 0, east)
                put(0, 0, west)
            elif dc == 2:
                put(1, 2, east)
                put(1, 4, west)
            else:
                put(0, 2, west)
                put(0, 4, east)
    sent_ref[20:38] = strips_ref[1 - side]
    kept_ref[20:38] = strips_ref[side]


def remap(side, dest, counts, ocean, land, weights, col_map, row_map, kappa, ga=12, gb=24):
    f32 = jnp.float32
    return pl.pallas_call(
        functools.partial(remap_kernel, ga=ga, gb=gb),
        out_shape=(jax.ShapeDtypeStruct((38, 8, 128), f32), jax.ShapeDtypeStruct((38, 8, 128), f32), jax.ShapeDtypeStruct((3, 208, 128), f32)),
        in_specs=[pl.BlockSpec(memory_space=pltpu.SMEM)] + [pl.BlockSpec(memory_space=pltpu.HBM)] * 8,
        out_specs=[pl.BlockSpec(memory_space=pltpu.VMEM)] * 3,
        scratch_shapes=[
            pltpu.SMEM((NBLK,), jnp.int32),
            pltpu.SMEM((1,), jnp.int32),
            pltpu.VMEM((F, OC), jnp.bfloat16),
            pltpu.VMEM((1, OC), jnp.int32),
            pltpu.VMEM((NBLK, BC, BR), jnp.bfloat16),
            pltpu.VMEM((NBLK, BC), jnp.int32),
            pltpu.VMEM((NBLK, BR), jnp.int32),
            pltpu.VMEM((AY, AX), f32),
            pltpu.VMEM((16, OC), f32),
            pltpu.VMEM((8, OC // 2), f32),
            pltpu.VMEM((192, 512), jnp.bfloat16),
            pltpu.VMEM((NBLK, 16, BR), f32),
            pltpu.VMEM((9, F * AY, AX), f32),
            pltpu.VMEM((2, 22, 8, BR), f32),
            pltpu.VMEM((2, 18, 8, AX), f32),
            pltpu.SMEM((9,), jnp.int32),
            pltpu.SemaphoreType.DMA((8,)),
        ],
        compiler_params=pltpu.CompilerParams(vmem_limit_bytes=32 * 1024 * 1024),
    )(side, counts, *[pltpu.with_memory_space_constraint(v, pltpu.HBM) for v in (dest, ocean, land, weights, col_map, row_map, kappa)])


def collect_kernel(place_ref, got_ref, mid_ref, far_ref, beside_ref, sent_ref, kept_ref, total_ref):
    f32, bf16, i32 = jnp.float32, jnp.bfloat16, jnp.int32
    core, side = place_ref[0], place_ref[1]
    main = 13 * AY
    total_ref[:, 0:main] = jnp.zeros((4, main, AX), f32)
    total_ref[pl.ds(core, 3), 0:main] = mid_ref[...]
    for q in range(4):
        for i in range(2):
            at = main + 8 * i
            total_ref[q, at:at + 8] = (got_ref[side, 40 + 2 * q + i] + far_ref[q, 8 * i:8 * i + 8]
                                       + beside_ref[q, 8 * i:8 * i + 8])
    lanes = lax.broadcasted_iota(i32, (AX, BR), 0)
    rows16 = lax.broadcasted_iota(i32, (AY, BR), 0)

    def factors(t, slot):
        base = 20 * t
        last = 4 * (slot % 2)
        value = jnp.concatenate([got_ref[side, base + slot], got_ref[side, base + 12 + slot // 2][last:last + 4]], 0)
        cell = got_ref[side, base + 18 + slot // 8][slot % 8:slot % 8 + 1].astype(i32)
        at_x = (lanes == jnp.bitwise_and(cell, AX - 1)).astype(f32).astype(bf16)
        at_y = rows16 == jnp.right_shift(cell, 7)
        head = value.astype(bf16).astype(f32)
        tail = value - head
        spread = lambda v: jnp.concatenate([jnp.where(at_y, v[f:f + 1, :], 0.0) for f in range(F)], 0).astype(bf16)
        return jnp.concatenate([spread(head), spread(tail)], 1), jnp.concatenate([at_x, at_x], 1)

    for q in range(4):
        slots = [(t, 4 * (q - t) + k) for t in range(2) if 0 <= q - t < 3 for k in range(4)]
        added = jnp.zeros((F * AY, AX), f32)
        for t, slot in slots:
            left, right = factors(t, slot)
            added = added + lax.dot_general(left, right, NT, preferred_element_type=f32)
        total_ref[q, 0:F * AY] = total_ref[q, 0:F * AY] + added
    kept_ref[...] = total_ref[pl.ds(2 * core, 2)]
    sent_ref[...] = total_ref[pl.ds(2 - 2 * core, 2)]


def collect(place, got, mid, far, beside):
    vm = pl.BlockSpec(memory_space=pltpu.VMEM)
    half = jax.ShapeDtypeStruct((2, 224, AX), jnp.float32)
    return pl.pallas_call(
        collect_kernel,
        out_shape=(half, half),
        in_specs=[pl.BlockSpec(memory_space=pltpu.SMEM), vm, vm, vm, vm],
        out_specs=(vm, vm),
        scratch_shapes=[pltpu.VMEM((4, 224, AX), jnp.float32)],
        compiler_params=pltpu.CompilerParams(vmem_limit_bytes=16 * 1024 * 1024),
    )(place, got, mid, far, beside)


SWEEPS = 3


def smooth_kernel(inside_ref, own_ref, top_ref, bottom_ref, out_ref, side_ref, main_ref, halo_ref):
    f32, i32 = jnp.float32, jnp.int32
    wide = 2 * AX
    tall = AY + 16
    strip = lambda a, a_at, b, b_at: jnp.concatenate([a[a_at:a_at + 8, :], b[b_at:b_at + 8, :]], 1)
    for slot, (west, east) in enumerate((
            (strip(own_ref, 208, own_ref, 216), strip(own_ref, 224, own_ref, 232)),
            (strip(bottom_ref, 104, top_ref, 104), strip(bottom_ref, 112, top_ref, 112)))):
        block = jnp.concatenate([east, jnp.zeros((AX - 16, wide), f32), west], 0)
        side_ref[slot, 0:AX] = block[:, :AX].T
        side_ref[slot, AX:wide] = block[:, AX:].T

    rows = lax.broadcasted_iota(i32, (tall, AX), 0)
    lane = lax.broadcasted_iota(i32, (24, AX), 1)
    inside = jnp.logical_and(jnp.logical_or(rows >= 8, inside_ref[2] == 1),
                             jnp.logical_or(rows < 8 + AY, inside_ref[3] == 1))
    for f in range(F + 1):
        keep = (lambda v, lo, hi: jnp.where(inside[lo:hi], v, 0.0)) if f < F else (lambda v, lo, hi: v)
        main_ref[f, 0:8] = keep(top_ref[8 * f:8 * f + 8], 0, 8)
        main_ref[f, 8:8 + AY] = own_ref[AY * f:AY * f + AY]
        main_ref[f, 8 + AY:tall] = keep(bottom_ref[8 * f:8 * f + 8], 8 + AY, tall)
        halo_ref[f, 0:8] = keep(side_ref[1, AX + 8 * f:AX + 8 * f + 8], 0, 8)
        halo_ref[f, 8:16] = side_ref[0, 8 * f:8 * f + 8]
        halo_ref[f, 16:24] = side_ref[0, AX + 8 * f:AX + 8 * f + 8]
        halo_ref[f, 8 + AY:tall] = keep(side_ref[1, 8 * f:8 * f + 8], 8 + AY, tall)

    def lap(ref, f, lo, n, own_rolls, other_rolls):
        at = lambda by: ref[f, lo + by:lo + by + n]
        size = lane[:n]
        turned = {by: jnp.where(size >= by if by > 0 else size < AX + by, own_rolls[by], other_rolls[by])
                  for by in (1, -1, 2, -2)}
        near = (at(-1) + at(1)) + (turned[1] + turned[-1])
        far = (at(-2) + at(2)) + (turned[2] + turned[-2])
        return 4.0 / 3.0 * near - 1.0 / 12.0 * far - 5.0 * at(0)

    for sweep in range(SWEEPS):
        last = sweep == SWEEPS - 1
        lo, n = (8, AY) if last else (4, 24)
        kappa_main, kappa_halo = main_ref[F, lo:lo + n], halo_ref[F, lo:lo + n]
        seen = inside[4:28]
        for f in range(F):
            u, v = main_ref[f, lo:lo + n], halo_ref[f, lo:lo + n]
            u_rolls = {by: pltpu.roll(u, by % AX, 1) for by in (1, -1, 2, -2)}
            v_rolls = {by: pltpu.roll(v, by % AX, 1) for by in (1, -1, 2, -2)}
            u = u + kappa_main * lap(main_ref, f, lo, n, u_rolls, v_rolls)
            if last:
                out_ref[f] = u
            else:
                v = v + kappa_halo * lap(halo_ref, f, lo, n, v_rolls, u_rolls)
                main_ref[f, lo:lo + n] = jnp.where(seen, u, 0.0)
                halo_ref[f, lo:lo + n] = jnp.where(seen, v, 0.0)


def smooth(inside, own, top, bottom):
    vm = pl.BlockSpec(memory_space=pltpu.VMEM)
    return pl.pallas_call(
        smooth_kernel,
        out_shape=jax.ShapeDtypeStruct((F, AY, AX), jnp.float32),
        in_specs=[pl.BlockSpec(memory_space=pltpu.SMEM), vm, vm, vm],
        out_specs=vm,
        scratch_shapes=[
            pltpu.VMEM((2, 2 * AX, AX), jnp.float32),
            pltpu.VMEM((F + 1, AY + 16, AX), jnp.float32),
            pltpu.VMEM((F + 1, AY + 16, AX), jnp.float32),
        ],
        compiler_params=pltpu.CompilerParams(vmem_limit_bytes=16 * 1024 * 1024),
    )(inside, own, top, bottom)


def partners(n_row, n_col):
    at = lambda r, c: (r % n_row) * n_col + c % n_col
    chip = [[at(2 * k, c), at(2 * k + 1, c)] for k in range(n_row // 2) for c in range(n_col)]
    beside = [[at(r, c), at(r, c + 1)] for r in range(n_row) for c in range(r % 2, n_col, 2)]
    bands = [[at(2 * k + 1, c), at(2 * k + 2, c)] for k in range(n_row // 2 - 1) for c in range(n_col)]
    bands += [[at(r, c), at(r, c + 1)] for r in (0, n_row - 1) for c in range(0, n_col, 2)]
    beyond = []
    for r in range(n_row):
        for c in range(n_col):
            step = 2 if (r + c) % 2 == 0 else -2
            beyond.append((at(r, c), at(r ^ 1, c + step)))
    return chip, beside, bands, beyond


def per_device(ocean, land, weights, col_map, row_map, dest, counts, kappa):
    both = ("row", "col")
    n_row, n_col = lax.axis_size("row"), lax.axis_size("col")
    chip, beside, bands, beyond = partners(n_row, n_col)
    row, col = lax.axis_index("row"), lax.axis_index("col")
    core = row % 2
    first = core == 0
    ahead = (row + col) % 2 == 0
    side = jnp.where(ahead, 1, 0).astype(jnp.int32)
    place = jnp.stack([v.astype(jnp.int32) for v in (core, side, row != 0, row != n_row - 1)])
    swap = lambda value, groups, place: lax.dynamic_index_in_dim(
        lax.all_gather(value, both, axis_index_groups=groups), place, 0, keepdims=False)
    take = lambda value, place: lax.dynamic_index_in_dim(value, place, 0, keepdims=False)
    part = lambda value, start, size, dim: lax.dynamic_slice_in_dim(value, start, size, dim)

    sent, mine, mid = remap(place, dest.reshape(NBLK), counts.reshape(1), ocean, land.reshape(1, OC), weights, col_map, row_map, kappa)
    other = swap(sent, chip, 1 - core)
    lower, upper = jnp.where(first, mine, other), jnp.where(first, other, mine)
    lift = lambda value, before: jnp.pad(value[20:].reshape(3, 48, AX), ((before, 1 - before), (0, 0), (0, 0)))
    strips = lift(lower, 0) + lift(upper, 1)
    far = lax.ppermute(strips[:, 16:32], both, beyond)
    near = lax.all_gather(jnp.concatenate([lower[:20], upper[:20], strips[:, 0:16].reshape(8, 8, AX)], 0),
                          both, axis_index_groups=beside)
    sent, mine = collect(place, near, mid, far, strips[:, 32:48])
    other = swap(sent, chip, 1 - core)
    east = jnp.where(ahead, mine[:, 208:], other[:, 208:])
    west = jnp.where(ahead, other[:, 208:], mine[:, 208:])
    main = mine[:, :208] + other[:, :208]
    half = lambda value, start: part(value[:208].reshape(13, AY, AX), start, 8, 1).reshape(104, AX)
    edges = jnp.concatenate([west, east], 1)
    mine_main, mine_edges = take(main, 1 - core), take(edges, 1 - core)
    out_main, out_edges = take(main, core), take(edges, core)
    half_edges = lambda value, place: part(value.reshape(2, 2, 8, AX), place, 1, 1).reshape(16, AX)
    main = F * AY
    sent = jnp.concatenate([out_main[:main], out_edges, half(mine_main, 8 * core), half_edges(mine_edges, core)], 0)
    got = swap(sent, bands, core)
    outer = jnp.logical_or(row == 0, row == n_row - 1)
    got = jnp.where(outer, 0.0, got)
    own = jnp.concatenate([mine_main[:main] + got[:main], mine_main[main:], mine_edges + got[main:main + 32]], 0)
    outside = jnp.concatenate([half(out_main, 8 - 8 * core), half_edges(out_edges, 1 - core)], 0) + got[main + 32:]
    within = swap(jnp.concatenate([half(own, 8 - 8 * core), half_edges(own[208:], 1 - core)], 0), chip, 1 - core)
    top = jnp.where(first, outside, within)
    bottom = jnp.where(first, within, outside)
    return smooth(place, own, top, bottom)


def solution(mesh):
    placed = (
        P("row", "col", None, None),
        P("row", "col", None),
        P("row", "col", None, None, None),
        P("row", "col", None, None),
        P("row", "col", None, None),
        P("row", "col", None, None),
        P("row", "col"),
        P("row", "col"),
    )
    return jax.shard_map(
        per_device, mesh=mesh, in_specs=placed, out_specs=P(None, "row", "col"), check_vma=False
    )
```
